256 devices in a mesh: lat: 64 (over z, x, y_lo), lon: 4 (over y_hi, core).
Axes of the slice: x: 4, y: 4 (y_hi: 2, y_lo: 2; y = y_hi * 2 + y_lo), z: 8, core: 2. Of those that a mesh axis runs over, the one named last changes fastest.
Arguments:
- tokens: bfloat16 [2, 384, 48, 512], P(None, 'lat', 'lon'), may hold values from -6 to 6
- land_sea: int32 [384, 48], P('lat', 'lon'), may hold values 0 or 1
- pole_band: int32 [384], P('lat'), may hold values 0 or 1
- land_embedding: bfloat16 [512], replicated, may hold values from -6 to 6
- pole_embedding: bfloat16 [512], replicated, may hold values from -6 to 6
- attend_first: bfloat16 [512, 1536], replicated, may hold values from -0.25 to 0.25
- output_first: bfloat16 [512, 512], replicated, may hold values from -0.5 to 0.5
- attend_second: bfloat16 [512, 1536], replicated, may hold values from -0.25 to 0.25
- output_second: bfloat16 [512, 512], replicated, may hold values from -0.5 to 0.5
- cotangent: bfloat16 [2, 384, 48, 512], P(None, 'lat', 'lon'), may hold values from -6 to 6
Outputs:
- layer_out: bfloat16 [2, 384, 48, 512], P(None, 'lat', 'lon')
- tokens_grad: bfloat16 [2, 384, 48, 512], P(None, 'lat', 'lon')
- grad_attend_first: float32 [512, 1536], P('lat')
- grad_output_first: float32 [512, 512], P('lat')
- grad_attend_second: float32 [512, 1536], P('lat')
- grad_output_second: float32 [512, 512], P('lat')
The draws below stay inside these ranges and needn't reach their ends.
All inputs are finite; a program needn't handle non-finite values. No bound on the sum of `land_sea` or of `pole_band` on one device may be relied on, other than what follows from the above.
Results may differ from the reference program's by a relative error of at most 0.02.
Values may be sent and summed in bfloat16 or wider, within the bound.
A program may use at most 128 MiB of HBM per device.

```python
import math
import jax
import jax.numpy as jnp
from jax import lax

D = 512
HEADS = 16
LV = 2
WLAT = 6
WLON = 12
NLAT = 384
NLON = 48


def set_ends(drawn, key, smallest, largest):
    longest = drawn.shape.index(max(drawn.shape))
    spots = []
    for shift in (0, 1):
        where = [jax.random.randint(jax.random.fold_in(key, axis), (), 0, length) for axis, length in enumerate(drawn.shape)]
        where[longest] = (where[longest] + shift) % drawn.shape[longest]
        spots.append(tuple(where))
    return drawn.at[spots[0]].set(smallest).at[spots[1]].set(largest)


def block_scale(key, shape, pieces, smallest, largest):
    loudness = 1.0
    for dim, parts in pieces:
        draws = jax.random.uniform(jax.random.fold_in(jax.random.fold_in(key, 6), dim), (parts,), jnp.float32, smallest / len(pieces), largest / len(pieces))
        loudness = loudness * jnp.repeat(jnp.exp(draws), shape[dim] // parts).reshape((-1,) + (1,) * (len(shape) - 1 - dim))
    return loudness


def scatter_about(own_key, dims, scale, most, pieces=(), dtype=jnp.bfloat16):
    gain = block_scale(own_key, dims, pieces, -0.22, 0.18) if pieces else 1.0
    drawn = jax.random.normal(own_key, dims, jnp.float32) * scale * gain
    return jnp.minimum(jnp.maximum(drawn, -most), most).astype(dtype)


def setup_inputs(seed: int = 0) -> dict:
    keys = jax.random.split(jax.random.key(seed), 11)
    tokens = scatter_about(keys[0], (LV, NLAT, NLON, D), 1.0, 6.0, ((1, 64), (2, 4)))
    land_sea = set_ends((jax.random.randint(keys[1], (NLAT, NLON), 0, 10) < 3).astype(jnp.int32), jax.random.fold_in(keys[1], 1), 0, 1)
    pole_band = set_ends((jax.random.randint(keys[2], (NLAT,), 0, 4) < 1).astype(jnp.int32), jax.random.fold_in(keys[2], 1), 0, 1)
    land_embedding = scatter_about(keys[3], (D,), 1.0, 6.0)
    pole_embedding = scatter_about(keys[4], (D,), 1.0, 6.0)
    attend_first = scatter_about(keys[5], (D, 3 * D), D ** -0.5, 0.25)
    output_first = scatter_about(keys[6], (D, D), (D // 4) ** -0.5, 0.5)
    attend_second = scatter_about(keys[7], (D, 3 * D), D ** -0.5, 0.25)
    output_second = scatter_about(keys[8], (D, D), (D // 4) ** -0.5, 0.5)
    cotangent = scatter_about(keys[9], (LV, NLAT, NLON, D), 1.0, 6.0, ((1, 64), (2, 4)))
    return {"tokens": tokens, "land_sea": land_sea, "pole_band": pole_band, "land_embedding": land_embedding, "pole_embedding": pole_embedding, "attend_first": attend_first, "output_first": output_first, "attend_second": attend_second, "output_second": output_second, "cotangent": cotangent}


EPS = 1e-05

def contract_rows(left, right):
    return lax.dot_general(left, right, (((0,), (0,)), ((), ())), preferred_element_type=jnp.float32)

def contract_cols(left, right):
    return lax.dot_general(left, right, (((1,), (1,)), ((), ())), preferred_element_type=jnp.float32)

def attend_forward(inputs, valid_keys, attend_weight, output_weight):
    window_count, window_size, features = inputs.shape
    per_head = features // HEADS
    centre = lax.optimization_barrier(jnp.mean(inputs, axis=-1, keepdims=True))
    centred = inputs - centre
    spread = lax.rsqrt(lax.optimization_barrier(jnp.mean(centred * centred, axis=-1, keepdims=True)) + EPS)
    normed = centred * spread
    hidden = normed.astype(jnp.bfloat16).reshape(window_count * window_size, features)
    packed = jnp.dot(hidden, attend_weight, preferred_element_type=jnp.float32).astype(jnp.bfloat16)
    packed = packed.reshape(window_count, window_size, 3, HEADS, per_head)
    query_part = packed[:, :, 0]
    key_part = packed[:, :, 1]
    value_part = packed[:, :, 2]
    scores = jnp.einsum('bqhd,bkhd->bhqk', query_part.astype(jnp.float32), key_part.astype(jnp.float32)) * (1.0 / math.sqrt(per_head))
    weights = jnp.exp(scores) * valid_keys[:, None, None, :]
    attention = weights / lax.optimization_barrier(jnp.sum(weights, axis=-1, keepdims=True))
    attention_low = attention.astype(jnp.bfloat16)
    mixed_heads = jnp.einsum('bhqk,bkhd->bqhd', attention_low.astype(jnp.float32), value_part.astype(jnp.float32))
    mixed_heads = mixed_heads.astype(jnp.bfloat16).reshape(window_count * window_size, features)
    outputs = inputs + jnp.dot(mixed_heads, output_weight, preferred_element_type=jnp.float32).reshape(window_count, window_size, features)
    return (outputs, (normed, spread, hidden, query_part, key_part, value_part, attention, attention_low, mixed_heads))

def attend_backward(saved, grad_out, keep_mask, attend_weight, output_weight):
    normed, spread, hidden, query_part, key_part, value_part, attention, attention_low, mixed_heads = saved
    window_count, window_size, features = grad_out.shape
    per_head = query_part.shape[3]
    grad_low = grad_out.astype(jnp.bfloat16)
    keep_low = keep_mask.astype(jnp.bfloat16)
    flat_grad = grad_low.reshape(window_count * window_size, features)
    kept_grad = (grad_low * keep_low[:, None, None]).reshape(window_count * window_size, features)
    output_grad = contract_rows(mixed_heads, kept_grad)
    grad_mixed = contract_cols(flat_grad, output_weight).astype(jnp.bfloat16)
    grad_mixed = grad_mixed.reshape(window_count, window_size, HEADS, per_head)
    grad_attention = jnp.einsum('bqhd,bkhd->bhqk', grad_mixed.astype(jnp.float32), value_part.astype(jnp.float32))
    grad_value = jnp.einsum('bhqk,bqhd->bkhd', attention_low.astype(jnp.float32), grad_mixed.astype(jnp.float32)).astype(jnp.bfloat16)
    inner = lax.optimization_barrier(jnp.sum(attention * grad_attention, axis=-1, keepdims=True))
    grad_scores = (attention * (grad_attention - inner) * (1.0 / math.sqrt(per_head))).astype(jnp.bfloat16)
    grad_query = jnp.einsum('bhqk,bkhd->bqhd', grad_scores.astype(jnp.float32), key_part.astype(jnp.float32)).astype(jnp.bfloat16)
    grad_key = jnp.einsum('bhqk,bqhd->bkhd', grad_scores.astype(jnp.float32), query_part.astype(jnp.float32)).astype(jnp.bfloat16)
    grad_packed = jnp.stack([grad_query, grad_key, grad_value], axis=2).reshape(window_count, window_size * 3 * features)
    kept_packed = (grad_packed * keep_low[:, None]).reshape(window_count * window_size, 3 * features)
    grad_packed = grad_packed.reshape(window_count * window_size, 3 * features)
    attend_grad = contract_rows(hidden, kept_packed)
    grad_hidden = contract_cols(grad_packed, attend_weight).reshape(window_count, window_size, features)
    grad_inputs = grad_out + spread * (grad_hidden - lax.optimization_barrier(jnp.mean(grad_hidden, axis=-1, keepdims=True)) - normed * lax.optimization_barrier(jnp.mean(grad_hidden * normed, axis=-1, keepdims=True)))
    return (grad_inputs, attend_grad, output_grad)

def partition(grid_field):
    levels, lat_rows, lon_cols, features = grid_field.shape
    blocks = grid_field.reshape(levels, lat_rows // WLAT, WLAT, lon_cols // WLON, WLON, features)
    blocks = blocks.transpose(1, 3, 0, 2, 4, 5)
    return blocks.reshape(lat_rows // WLAT, lon_cols // WLON, levels * WLAT * WLON, features)

def assemble(blocks, levels):
    band_count, sector_count, window_size, features = blocks.shape
    grid = blocks.reshape(band_count, sector_count, levels, WLAT, WLON, features)
    return grid.transpose(2, 0, 3, 1, 4, 5).reshape(levels, band_count * WLAT, sector_count * WLON, features)

def run_forward(blocks, valid_keys, attend_weight, output_weight):

    def advance(totals, slices):
        outputs, unused = attend_forward(slices[0], slices[1], attend_weight, output_weight)
        return (totals, outputs)
    unused_total, outputs = lax.scan(advance, jnp.zeros((), jnp.float32), (blocks, valid_keys))
    return outputs

def run_both(blocks, valid_keys, grad_blocks, attend_weight, output_weight):
    features = blocks.shape[-1]
    starting = (jnp.zeros((features, 3 * features), jnp.float32), jnp.zeros((features, features), jnp.float32))

    def advance(totals, slices):
        outputs, saved = attend_forward(slices[0], slices[1], attend_weight, output_weight)
        keep_mask = jnp.ones((slices[0].shape[0],), jnp.float32)
        grad_inputs, attend_grad, output_grad = attend_backward(saved, slices[2], keep_mask, attend_weight, output_weight)
        return ((totals[0] + attend_grad, totals[1] + output_grad), (outputs, grad_inputs))
    totals, results = lax.scan(advance, starting, (blocks, valid_keys, grad_blocks))
    return (totals, results)

def reference(tokens, land_sea, pole_band, land_embedding, pole_embedding, attend_first, output_first, attend_second, output_second, cotangent):
    levels = tokens.shape[0]
    marked = (tokens.astype(jnp.float32) + land_sea.astype(jnp.float32)[None, :, :, None] * land_embedding.astype(jnp.float32) + pole_band.astype(jnp.float32)[None, :, None, None] * pole_embedding.astype(jnp.float32)).astype(jnp.bfloat16)
    first_blocks = partition(marked.astype(jnp.float32))
    first_valid = jnp.ones(first_blocks.shape[:3], jnp.float32)
    first = assemble(run_forward(first_blocks, first_valid, attend_first, output_first), levels).astype(jnp.bfloat16)
    half_lat = WLAT // 2
    half_lon = WLON // 2

    def shift_in(grid_field):
        padded = jnp.pad(grid_field, ((0, 0), (half_lat, half_lat), (0, 0), (0, 0)))
        return jnp.roll(padded, half_lon, axis=2)

    def shift_out(grid_field):
        return jnp.roll(grid_field, -half_lon, axis=2)[:, half_lat:half_lat + NLAT]
    padded_rows = NLAT + WLAT
    row_index = jnp.arange(padded_rows)
    present = ((row_index >= half_lat) & (row_index < half_lat + NLAT)).astype(jnp.float32)
    present_field = jnp.broadcast_to(present[None, :, None, None], (levels, padded_rows, NLON, 1))
    second_valid = partition(present_field)[..., 0]
    second_blocks = partition(shift_in(first).astype(jnp.float32))
    second_grads = partition(shift_in(cotangent).astype(jnp.float32))
    second_totals, second_results = run_both(second_blocks, second_valid, second_grads, attend_second, output_second)
    layer_out = shift_out(assemble(second_results[0], levels)).astype(jnp.bfloat16)
    carried = shift_out(assemble(second_results[1], levels))
    first_totals, first_results = run_both(first_blocks, first_valid, partition(carried), attend_first, output_first)
    tokens_grad = assemble(first_results[1], levels).astype(jnp.bfloat16)
    return (layer_out, tokens_grad, first_totals[0], first_totals[1], second_totals[0], second_totals[1])
```

```python
import functools
import math

import jax
import jax.numpy as jnp
from jax import lax
from jax.experimental import pallas as pl
from jax.experimental.pallas import tpu as pltpu
from jax.sharding import PartitionSpec as P

MESH = pl.DeviceIdType.MESH
BF16 = jnp.bfloat16
F32 = jnp.float32

D = 512
HEADS = 16
PER_HEAD = D // HEADS
LV = 2
WLAT = 6
WLON = 12
CELLS = LV * WLAT * WLON
QUAD = CELLS // 4
SLAB = 48
EPS = 1e-05
SCALE = 1.0 / math.sqrt(PER_HEAD)
EXP2_SCALE = SCALE * math.log2(math.e)

NZ, NX, NYL = 8, 4, 2


def mm(left, right):
    return lax.dot_general(left, right, (((1,), (0,)), ((), ())), preferred_element_type=F32)


def mm_nt(left, right):
    return lax.dot_general(left, right, (((1,), (1,)), ((), ())), preferred_element_type=F32)


def quadrant(row, side):
    return (0 if row >= 3 else 1) + (0 if side == 1 else 2)


def chunk_offset(level, row, side):
    return quadrant(row, side) * QUAD + (level * 3 + row % 3) * 6


def slabs_to_cells(slab_ref, cells_ref):
    for level in range(LV):
        for row in range(WLAT):
            for side in range(2):
                off = chunk_offset(level, row, side)
                cells_ref[off : off + 6, :] = slab_ref[level * WLAT + row, side * 6 : side * 6 + 6, :]


def cells_to_field(cells_ref, slab_ref, field_ref):
    for level in range(LV):
        for row in range(WLAT):
            for side in range(2):
                off = chunk_offset(level, row, side)
                slab_ref[level * WLAT + row, side * 6 : side * 6 + 6, :] = cells_ref[off : off + 6, :]
            field_ref[level, row, :, :] = slab_ref[level * WLAT + row, 0:WLON, :].astype(BF16)


def layer_norm(u):
    centre = jnp.mean(u, axis=-1, keepdims=True)
    centred = u - centre
    spread = lax.rsqrt(jnp.mean(centred * centred, axis=-1, keepdims=True) + EPS)
    return centred * spread, spread


def head_lanes(head):
    lane = lax.broadcasted_iota(jnp.int32, (CELLS, 256), 1)
    return (lane // PER_HEAD) == (head % 8)


def forward(blk, w_ref, wo_ref, mask_ref):
    u = blk.u[...]
    normed, spread = layer_norm(u)
    blk.normed[...] = normed
    blk.spread[...] = jnp.broadcast_to(spread, (CELLS, 128))
    hidden = normed.astype(BF16)
    blk.hid_t[...] = hidden.T
    for part in range(3):
        cols = slice(part * D, part * D + D)
        packed = mm(hidden, w_ref[:, cols]).astype(BF16)
        blk.pk[:, cols] = packed
        blk.pk_t[cols, :] = packed.T

    def one_head(head):
        group = head // 8
        q_g = blk.pk[:, group * 256 : group * 256 + 256]
        k_g = blk.pk[:, D + group * 256 : D + group * 256 + 256]
        k_h = jnp.where(head_lanes(head), k_g, jnp.zeros_like(k_g))
        weights = jnp.exp2(mm_nt(k_h, q_g) * EXP2_SCALE)
        if mask_ref is not None:
            weights = weights * mask_ref[...]
        attention = (weights * (1.0 / jnp.sum(weights, axis=0, keepdims=True))).astype(BF16)
        blk.att[head] = attention
        rows = slice(head * PER_HEAD, head * PER_HEAD + PER_HEAD)
        v_t = blk.pk_t[2 * D + head * PER_HEAD : 2 * D + head * PER_HEAD + PER_HEAD, :]
        blk.mix_t[rows, :] = mm(v_t, attention)

    for head in range(HEADS):
        one_head(head)
    mixed = blk.mix_t[...].astype(BF16).T
    return u + mm(mixed, wo_ref[...])


def backward_heads(blk, wo_ref):
    dy_low = blk.dy[...].astype(BF16)
    blk.gm[...] = mm_nt(dy_low, wo_ref[...]).astype(BF16)
    blk.gm_t[...] = blk.gm[...].T

    def one_head(head):
        group = head // 8
        v_g = blk.pk[:, 2 * D + group * 256 : 2 * D + group * 256 + 256]
        g_g = blk.gm[:, group * 256 : group * 256 + 256]
        v_h = jnp.where(head_lanes(head), v_g, jnp.zeros_like(v_g))
        grad_attention = mm_nt(v_h, g_g)
        rows = slice(head * PER_HEAD, head * PER_HEAD + PER_HEAD)
        g_t = blk.gm_t[rows, :]
        inner = jnp.sum(blk.mix_t[rows, :] * g_t.astype(F32), axis=0, keepdims=True)
        attention = blk.att[head]
        grad_scores = (attention.astype(F32) * (grad_attention - inner)).astype(BF16)
        q_t = blk.pk_t[rows, :]
        k_t = blk.pk_t[D + head * PER_HEAD : D + head * PER_HEAD + PER_HEAD, :]
        blk.dpk_t[2 * D + head * PER_HEAD : 2 * D + head * PER_HEAD + PER_HEAD, :] = mm_nt(g_t, attention).astype(BF16)
        blk.dpk_t[rows, :] = (mm(k_t, grad_scores) * SCALE).astype(BF16)
        blk.dpk_t[D + head * PER_HEAD : D + head * PER_HEAD + PER_HEAD, :] = (mm_nt(q_t, grad_scores) * SCALE).astype(BF16)

    for head in range(HEADS):
        one_head(head)


def backward_input(blk, w_ref):
    grad_hidden = mm(w_ref[...], blk.dpk_t[...]).T
    normed = blk.normed[...]
    spread = blk.spread[:, 0:1]
    return blk.dy[...] + spread * (
        grad_hidden
        - jnp.mean(grad_hidden, axis=-1, keepdims=True)
        - normed * jnp.mean(grad_hidden * normed, axis=-1, keepdims=True)
    )


def pack_unit(first, second):
    first = first.reshape(64, 8, D)
    second = second.reshape(64, 8, D)
    return jnp.concatenate([first, second], axis=1).astype(BF16).reshape(NZ, NX, NYL, 16, D)


def output_and_value_unit(blk):
    grad_output = mm(blk.mix_t[...].astype(BF16), blk.dy[...].astype(BF16))
    grad_value = mm_nt(blk.hid_t[...], blk.dpk_t[2 * D :, :])
    return pack_unit(grad_output, grad_value)


def query_and_key_unit(blk):
    hid_t = blk.hid_t[...]
    return pack_unit(mm_nt(hid_t, blk.dpk_t[0:D, :]), mm_nt(hid_t, blk.dpk_t[D : 2 * D, :]))


BLOCK_SCRATCH = (
    ("u", (CELLS, D), F32),
    ("normed", (CELLS, D), F32),
    ("spread", (CELLS, 128), F32),
    ("hid_t", (D, CELLS), BF16),
    ("pk", (CELLS, 3 * D), BF16),
    ("pk_t", (3 * D, CELLS), BF16),
    ("att", (HEADS, CELLS, CELLS), BF16),
    ("mix_t", (D, CELLS), F32),
    ("dy", (CELLS, D), F32),
    ("gm", (CELLS, D), BF16),
    ("gm_t", (D, CELLS), BF16),
    ("dpk_t", (3 * D, CELLS), BF16),
)


class Block:
    def __init__(self, refs):
        for (name, _, _), ref in zip(BLOCK_SCRATCH, refs):
            setattr(self, name, ref)


class Torus:
    def __init__(self):
        self.lat = lax.axis_index("lat")
        self.lon = lax.axis_index("lon")
        self.z = self.lat // 8
        self.x = (self.lat // 2) % 4
        self.y = (self.lon // 2) * 2 + self.lat % 2
        self.core = self.lon % 2

    def at(self, x=None, y=None, z=None, core=None):
        x = self.x if x is None else x
        y = self.y if y is None else y
        z = self.z if z is None else z
        core = self.core if core is None else core
        return (z * 8 + x * 2 + y % 2, (y // 2) * 2 + core)

    def shifted(self, dlat, dlon):
        return ((self.lat + dlat + 64) % 64, (self.lon + dlon + 4) % 4)

    def greeted(self):
        found = [self.shifted(*step) for step in ((1, 0), (-1, 0), (1, 1), (-1, -1), (0, 1), (0, 2), (0, 3))]
        found += [self.at(y=(self.y + k) % 4) for k in (1, 3)]
        found += [self.at(x=(self.x + k) % 4) for k in (1, 2, 3)]
        found += [self.at(z=(self.z + k) % 8) for k in range(1, 8)]
        return found


class Halo:
    STEPS = ((1, 0), (0, 1), (1, 1))

    def __init__(self, torus, index, sign, out_ref, in_ref, send_sem, recv_sem):
        self.out_ref = out_ref.at[index]
        self.in_ref = in_ref.at[index]
        self.copies = [
            pltpu.make_async_remote_copy(
                src_ref=out_ref.at[index, n],
                dst_ref=in_ref.at[index, n],
                send_sem=send_sem.at[index, n],
                recv_sem=recv_sem.at[index, n],
                device_id=torus.shifted(sign * step[0], sign * step[1]),
                device_id_type=MESH,
            )
            for n, step in enumerate(self.STEPS)
        ]

    def send(self, cells_ref):
        for n, copy in enumerate(self.copies):
            q = n + 1
            self.out_ref[n, 0:QUAD, :] = cells_ref[q * QUAD : q * QUAD + QUAD, :].astype(BF16)
            copy.start()

    def receive(self, cells_ref):
        for n, copy in enumerate(self.copies):
            q = n + 1
            copy.wait_recv()
            cells_ref[q * QUAD : q * QUAD + QUAD, :] = self.in_ref[n, 0:QUAD, :].astype(F32)

    def close(self):
        for copy in self.copies:
            copy.wait_send()


REDUCE_SCRATCH = (
    ("whole", (4, NZ, NX, NYL, 16, D), BF16),
    ("core_in", (4, NZ, NX, NYL, 16, 256), BF16),
    ("s1", (4, NZ, NX, NYL, 16, 256), BF16),
    ("ya_in", (2, 3, NZ, NX, 16, 128), BF16),
    ("ya_sum", (2, NZ, NX, 16, 128), BF16),
    ("xa_in", (2, 3, NZ, 16, 128), BF16),
    ("xb_in", (2, 3, NZ, NYL, 16, 256), BF16),
    ("xb_sum", (2, NZ, NYL, 16, 256), BF16),
    ("yb_in", (2, 3, NZ, 16, 128), BF16),
    ("s3", (4, NZ, 16, 128), BF16),
    ("z_in", (4, 7, 16, 128), BF16),
    ("last", (4, 4, 16, 128), F32),
)
REDUCE_SEMS = 17


class Reduce:
    def __init__(self, torus, unit, bufs, send_sem, recv_sem):
        self.t, self.unit, self.b = torus, unit, bufs
        self.send_sem, self.recv_sem = send_sem.at[unit], recv_sem.at[unit]
        self.y_first = unit % 2 == 0
        self.half = unit // 2
        self.pending = []

    def _copy(self, src, dst, sem_out, sem_in, device):
        copy = pltpu.make_async_remote_copy(
            src_ref=src,
            dst_ref=dst,
            send_sem=self.send_sem.at[sem_out],
            recv_sem=self.recv_sem.at[sem_in],
            device_id=device,
            device_id_type=MESH,
        )
        copy.start()
        self.pending.append(copy)
        return copy

    def _axis(self, size, base, pick, landing, device):
        self.arriving = []
        for k in range(1, size):
            slot = size - k - 1
            self.arriving.append(self._copy(pick(k), landing.at[slot], base + slot, base + slot, device(k)))

    def _arrived(self):
        for copy in self.arriving:
            copy.wait_recv()

    def start(self):
        t, b, u = self.t, self.b, self.unit
        cols = pl.ds(pl.multiple_of((1 - t.core) * 256, 256), 256)
        self.arriving = [
            self._copy(b.whole.at[u, :, :, :, :, cols], b.core_in.at[u], 0, 0, t.at(core=1 - t.core))
        ]

    def _send_y(self, pick):
        t, b = self.t, self.b
        landing = b.ya_in.at[self.half] if self.y_first else b.yb_in.at[self.half]
        self._axis(4, 1, pick, landing, lambda k: t.at(y=(t.y + k) % 4))

    def _send_x(self, pick):
        t, b = self.t, self.b
        landing = b.xa_in.at[self.half] if self.y_first else b.xb_in.at[self.half]
        self._axis(4, 4, pick, landing, lambda k: t.at(x=(t.x + k) % 4))

    def _y_cols(self, k):
        return pl.ds(pl.multiple_of(((self.t.y + k) % 4) // 2 * 128, 128), 128)

    def after_core(self):
        t, b, u = self.t, self.b, self.unit
        self._arrived()
        cols = pl.ds(pl.multiple_of(t.core * 256, 256), 256)
        b.s1[u] = (b.whole[u, :, :, :, :, cols].astype(F32) + b.core_in[u].astype(F32)).astype(BF16)
        if self.y_first:
            self._send_y(lambda k: b.s1.at[u, :, :, (t.y + k) % 2, :, self._y_cols(k)])
        else:
            self._send_x(lambda k: b.s1.at[u, :, (t.x + k) % 4])

    def after_first(self):
        t, b, u, h = self.t, self.b, self.unit, self.half
        self._arrived()
        if self.y_first:
            total = b.s1[u, :, :, t.y % 2, :, self._y_cols(0)].astype(F32)
            for n in range(3):
                total = total + b.ya_in[h, n].astype(F32)
            b.ya_sum[h] = total.astype(BF16)
            self._send_x(lambda k: b.ya_sum.at[h, :, (t.x + k) % 4])
        else:
            total = b.s1[u, :, t.x].astype(F32)
            for n in range(3):
                total = total + b.xb_in[h, n].astype(F32)
            b.xb_sum[h] = total.astype(BF16)
            self._send_y(lambda k: b.xb_sum.at[h, :, (t.y + k) % 2, :, self._y_cols(k)])

    def after_second(self):
        t, b, u, h = self.t, self.b, self.unit, self.half
        self._arrived()
        if self.y_first:
            total, came = b.ya_sum[h, :, t.x].astype(F32), b.xa_in
        else:
            total, came = b.xb_sum[h, :, t.y % 2, :, self._y_cols(0)].astype(F32), b.yb_in
        for n in range(3):
            total = total + came[h, n].astype(F32)
        b.s3[u] = total.astype(BF16)
        self._axis(8, 7, lambda k: b.s3.at[u, (t.z + k) % 8], b.z_in.at[u], lambda k: t.at(z=(t.z + k) % 8))

    def after_z(self):
        t, b, u = self.t, self.b, self.unit
        self._arrived()
        total = b.s3[u, t.z].astype(F32)
        for n in range(7):
            total = total + b.z_in[u, n].astype(F32)
        b.last[u, t.lon] = total
        self.arriving = []
        for k in range(1, 4):
            slot = 4 - k - 1
            self.arriving.append(
                self._copy(b.last.at[u, t.lon], b.last.at[u, t.lon], 14 + slot, 14 + slot, t.shifted(0, k))
            )

    def finish(self, first_ref, first_col, second_ref, second_col):
        b, u = self.b, self.unit
        self._arrived()
        for lon in range(4):
            off = (lon % 2) * 256 + (lon // 2) * 128
            first_ref[:, first_col + off : first_col + off + 128] = b.last[u, lon, 0:8, :]
            second_ref[:, second_col + off : second_col + off + 128] = b.last[u, lon, 8:16, :]

    def close(self):
        for copy in self.pending:
            copy.wait_send()


class Named:
    pass


def kernel(
    tokens_ref,
    land_ref,
    pole_ref,
    land_vec_ref,
    pole_vec_ref,
    w1_hbm,
    o1_hbm,
    w2_hbm,
    o2_hbm,
    cot_ref,
    layer_ref,
    tokens_grad_ref,
    ga1_ref,
    go1_ref,
    ga2_ref,
    go2_ref,
    *scratch,
):
    n = len(BLOCK_SCRATCH)
    one, two = Block(scratch[:n]), Block(scratch[n : 2 * n])
    bufs = Named()
    for (name, _, _), ref in zip(REDUCE_SCRATCH, scratch[2 * n :]):
        setattr(bufs, name, ref)
    (w1_ref, o1_ref, w2_ref, o2_ref, slab_ref, cells_ref, mask_ref, halo_out, halo_in, load_sem, halo_send, halo_recv,
     red_send, red_recv) = scratch[2 * n + len(REDUCE_SCRATCH) :]

    torus = Torus()
    barrier = pltpu.get_barrier_semaphore()
    greeted = torus.greeted()
    for device in greeted:
        pl.semaphore_signal(barrier, inc=1, device_id=device, device_id_type=MESH)

    loads = [
        pltpu.make_async_copy(src, dst, load_sem.at[i])
        for i, (src, dst) in enumerate(((w1_hbm, w1_ref), (o1_hbm, o1_ref), (w2_hbm, w2_ref), (o2_hbm, o2_ref)))
    ]
    for load in loads:
        load.start()

    land = land_ref[...].astype(F32)
    eye = lax.broadcasted_iota(jnp.int32, (WLON, WLON), 0) == lax.broadcasted_iota(jnp.int32, (WLON, WLON), 1)
    land_vec = land_vec_ref[...].astype(F32)
    pole_vec = pole_vec_ref[...].astype(F32)
    for row in range(WLAT):
        marks = jnp.broadcast_to(land[row : row + 1, :], (WLON, WLON))
        column = jnp.sum(jnp.where(eye, marks, 0.0), axis=1, keepdims=True)
        on_land = column * land_vec
        polar = pole_ref[row].astype(F32) * pole_vec
        for level in range(LV):
            marked = tokens_ref[level, row, :, :].astype(F32) + on_land + polar
            slab_ref[level * WLAT + row, 0:WLON, :] = marked.astype(BF16).astype(F32)
    slabs_to_cells(slab_ref, one.u)

    for row in range(WLAT):
        for level in range(LV):
            slab_ref[level * WLAT + row, 0:WLON, :] = cot_ref[level, row, :, :].astype(F32)
    slabs_to_cells(slab_ref, two.dy)

    last = jnp.where(torus.lat == 63, 1.0, 0.0).astype(F32)
    far_k = (lax.broadcasted_iota(jnp.int32, (CELLS, CELLS), 0) // QUAD) % 2
    far_q = (lax.broadcasted_iota(jnp.int32, (CELLS, CELLS), 1) // QUAD) % 2
    mask_ref[...] = 1.0 - last * jnp.where(far_k == far_q, 0.0, 1.0)

    halos = [
        Halo(torus, i, sign, halo_out, halo_in, halo_send, halo_recv) for i, sign in enumerate((-1, -1, 1, 1))
    ]
    units = [Reduce(torus, u, bufs, red_send, red_recv) for u in range(4)]

    loads[0].wait()
    loads[1].wait()
    first = forward(one, w1_ref, o1_ref, None)
    two.u[...] = first.astype(BF16).astype(F32)

    pl.semaphore_wait(barrier, len(greeted))
    halos[0].send(two.u)
    halos[1].send(two.dy)
    loads[2].wait()
    loads[3].wait()
    halos[0].receive(two.u)
    cells_ref[...] = forward(two, w2_ref, o2_ref, mask_ref)
    halos[2].send(cells_ref)
    halos[1].receive(two.dy)

    backward_heads(two, o2_ref)
    one.dy[...] = backward_input(two, w2_ref)
    halos[3].send(one.dy)
    bufs.whole[0] = output_and_value_unit(two)
    units[0].start()
    bufs.whole[1] = query_and_key_unit(two)
    units[1].start()

    halos[3].receive(one.dy)
    units[0].after_core()
    backward_heads(one, o1_ref)
    units[1].after_core()
    bufs.whole[2] = output_and_value_unit(one)
    units[2].start()
    bufs.whole[3] = query_and_key_unit(one)
    units[3].start()
    units[0].after_first()
    units[1].after_first()

    halos[2].receive(cells_ref)
    cells_to_field(cells_ref, slab_ref, layer_ref)
    units[2].after_core()
    units[3].after_core()
    units[0].after_second()
    units[1].after_second()
    cells_ref[...] = backward_input(one, w1_ref)
    cells_to_field(cells_ref, slab_ref, tokens_grad_ref)
    units[2].after_first()
    units[3].after_first()
    units[0].after_z()
    units[1].after_z()
    units[2].after_second()
    units[3].after_second()
    units[0].finish(go2_ref, 0, ga2_ref, 2 * D)
    units[1].finish(ga2_ref, 0, ga2_ref, D)
    units[2].after_z()
    units[3].after_z()
    units[2].finish(go1_ref, 0, ga1_ref, 2 * D)
    units[3].finish(ga1_ref, 0, ga1_ref, D)
    for halo in halos:
        halo.close()
    for unit in units:
        unit.close()


def local(
    tokens,
    land_sea,
    pole_band,
    land_embedding,
    pole_embedding,
    attend_first,
    output_first,
    attend_second,
    output_second,
    cotangent,
):
    vmem = pl.BlockSpec(memory_space=pltpu.VMEM)
    smem = pl.BlockSpec(memory_space=pltpu.SMEM)
    hbm = pl.BlockSpec(memory_space=pl.ANY)
    field = jax.ShapeDtypeStruct(tokens.shape, BF16)
    return pl.pallas_call(
        kernel,
        out_shape=(
            field,
            field,
            jax.ShapeDtypeStruct((8, 3 * D), F32),
            jax.ShapeDtypeStruct((8, D), F32),
            jax.ShapeDtypeStruct((8, 3 * D), F32),
            jax.ShapeDtypeStruct((8, D), F32),
        ),
        in_specs=[vmem, vmem, smem, vmem, vmem, hbm, hbm, hbm, hbm, vmem],
        out_specs=[vmem] * 6,
        scratch_shapes=[pltpu.VMEM(shape, dtype) for _, shape, dtype in BLOCK_SCRATCH * 2 + REDUCE_SCRATCH]
        + [
            pltpu.VMEM((D, 3 * D), BF16),
            pltpu.VMEM((D, D), BF16),
            pltpu.VMEM((D, 3 * D), BF16),
            pltpu.VMEM((D, D), BF16),
            pltpu.VMEM((LV * WLAT, 16, D), F32),
            pltpu.VMEM((CELLS, D), F32),
            pltpu.VMEM((CELLS, CELLS), F32),
            pltpu.VMEM((4, 3, SLAB, D), BF16),
            pltpu.VMEM((4, 3, SLAB, D), BF16),
            pltpu.SemaphoreType.DMA((4,)),
            pltpu.SemaphoreType.DMA((4, 3)),
            pltpu.SemaphoreType.DMA((4, 3)),
            pltpu.SemaphoreType.DMA((4, REDUCE_SEMS)),
            pltpu.SemaphoreType.DMA((4, REDUCE_SEMS)),
        ],
        compiler_params=pltpu.CompilerParams(
            collective_id=0, has_side_effects=True, vmem_limit_bytes=56 * 1024 * 1024
        ),
    )(
        tokens,
        land_sea,
        pole_band,
        land_embedding.reshape(1, D),
        pole_embedding.reshape(1, D),
        attend_first,
        output_first,
        attend_second,
        output_second,
        cotangent,
    )


def solution(mesh):
    placed = (
        P(None, "lat", "lon", None),
        P("lat", "lon"),
        P("lat"),
        P(),
        P(),
        P(),
        P(),
        P(),
        P(),
        P(None, "lat", "lon", None),
    )
    return jax.shard_map(
        local,
        mesh=mesh,
        in_specs=placed,
        out_specs=(
            P(None, "lat", "lon", None),
            P(None, "lat", "lon", None),
            P("lat", None),
            P("lat", None),
            P("lat", None),
            P("lat", None),
        ),
        check_vma=False,
    )
```

```python
import functools
import math

import jax
import jax.numpy as jnp
from jax import lax
from jax.experimental import pallas as pl
from jax.experimental.pallas import tpu as pltpu
from jax.sharding import PartitionSpec as P

MESH = pl.DeviceIdType.MESH
BF16 = jnp.bfloat16
F32 = jnp.float32

D = 512
HEADS = 16
PER_HEAD = D // HEADS
LV = 2
WLAT = 6
WLON = 12
CELLS = LV * WLAT * WLON
QUAD = CELLS // 4
SLAB = 48
EPS = 1e-05
SCALE = 1.0 / math.sqrt(PER_HEAD)
EXP2_SCALE = SCALE * math.log2(math.e)

NZ, NX, NYL = 8, 4, 2
PLANE = [(dx, dy) for dx in (2, 1, 3, 0) for dy in (2, 1, 3, 0) if (dx, dy) != (0, 0)]
COLUMN = [(dz, dh) for dz in (4, 3, 5, 2, 6, 1, 7, 0) for dh in (1, 0) if (dz, dh) != (0, 0)]


def mm(left, right):
    return lax.dot_general(left, right, (((1,), (0,)), ((), ())), preferred_element_type=F32)


def mm_nt(left, right):
    return lax.dot_general(left, right, (((1,), (1,)), ((), ())), preferred_element_type=F32)


def chunk_offset(row, side):
    quadrant = (0 if row >= 3 else 1) + (0 if side == 1 else 2)
    return quadrant * QUAD + row % 3 * 12


def field_to_cells(field_ref, cells_ref, change=lambda chunk, row, side: chunk):
    for row in range(WLAT):
        for side in range(2):
            off = chunk_offset(row, side)
            chunk = field_ref[row, side * 6 : side * 6 + 6, :, :].astype(F32)
            cells_ref[off : off + 12, :] = change(chunk, row, side).reshape(12, D)


def cells_to_field(cells_ref, field_ref):
    for row in range(WLAT):
        for side in range(2):
            off = chunk_offset(row, side)
            field_ref[row, side * 6 : side * 6 + 6, :, :] = cells_ref[off : off + 12, :].reshape(6, LV, D).astype(BF16)


def layer_norm(u):
    centre = jnp.mean(u, axis=-1, keepdims=True)
    centred = u - centre
    spread = lax.rsqrt(jnp.mean(centred * centred, axis=-1, keepdims=True) + EPS)
    return centred * spread, spread


def head_lanes(head):
    lane = lax.broadcasted_iota(jnp.int32, (CELLS, 256), 1)
    return (lane // PER_HEAD) == (head % 8)


def forward(blk, w_ref, wo_ref, mask_ref):
    u = blk.u[...]
    normed, spread = layer_norm(u)
    blk.normed[...] = normed
    blk.spread[...] = jnp.broadcast_to(spread, (CELLS, 128))
    hidden = normed.astype(BF16)
    blk.hid_t[...] = hidden.T
    for part in range(3):
        cols = slice(part * D, part * D + D)
        packed = mm(hidden, w_ref[:, cols]).astype(BF16)
        blk.pk[:, cols] = packed
        blk.pk_t[cols, :] = packed.T

    def one_head(head):
        group = head // 8
        q_g = blk.pk[:, group * 256 : group * 256 + 256]
        k_g = blk.pk[:, D + group * 256 : D + group * 256 + 256]
        k_h = jnp.where(head_lanes(head), k_g, jnp.zeros_like(k_g))
        weights = jnp.exp2(mm_nt(k_h, q_g) * EXP2_SCALE)
        if mask_ref is not None:
            weights = weights * mask_ref[...]
        attention = (weights * (1.0 / jnp.sum(weights, axis=0, keepdims=True))).astype(BF16)
        blk.att[head] = attention
        rows = slice(head * PER_HEAD, head * PER_HEAD + PER_HEAD)
        v_t = blk.pk_t[2 * D + head * PER_HEAD : 2 * D + head * PER_HEAD + PER_HEAD, :]
        blk.mix_t[rows, :] = mm(v_t, attention)

    for head in range(HEADS):
        one_head(head)
    mixed = blk.mix_t[...].astype(BF16).T
    return u + mm(mixed, wo_ref[...])


def head_rows(part, head):
    first = part * D + head * PER_HEAD
    return slice(first, first + PER_HEAD)


def backward_values(blk, wo_ref):
    dy_low = blk.dy[...].astype(BF16)
    blk.gm[...] = mm_nt(dy_low, wo_ref[...]).astype(BF16)
    blk.gm_t[...] = blk.gm[...].T
    for head in range(HEADS):
        g_t = blk.gm_t[head_rows(0, head), :]
        blk.dpk_t[head_rows(2, head), :] = mm_nt(g_t, blk.att[head]).astype(BF16)


def backward_scores(blk, heads):
    for head in heads:
        group = head // 8
        v_g = blk.pk[:, 2 * D + group * 256 : 2 * D + group * 256 + 256]
        g_g = blk.gm[:, group * 256 : group * 256 + 256]
        v_h = jnp.where(head_lanes(head), v_g, jnp.zeros_like(v_g))
        grad_attention = mm_nt(v_h, g_g)
        rows = head_rows(0, head)
        g_t = blk.gm_t[rows, :]
        inner = jnp.sum(blk.mix_t[rows, :] * g_t.astype(F32), axis=0, keepdims=True)
        grad_scores = (blk.att[head].astype(F32) * (grad_attention - inner)).astype(BF16)
        q_t = blk.pk_t[rows, :]
        k_t = blk.pk_t[head_rows(1, head), :]
        blk.dpk_t[rows, :] = (mm(k_t, grad_scores) * SCALE).astype(BF16)
        blk.dpk_t[head_rows(1, head), :] = (mm_nt(q_t, grad_scores) * SCALE).astype(BF16)


def backward_input(blk, w_ref):
    grad_hidden = mm(w_ref[...], blk.dpk_t[...]).T
    normed = blk.normed[...]
    spread = blk.spread[:, 0:1]
    return blk.dy[...] + spread * (
        grad_hidden
        - jnp.mean(grad_hidden, axis=-1, keepdims=True)
        - normed * jnp.mean(grad_hidden * normed, axis=-1, keepdims=True)
    )


def pack_unit(first, second):
    first = first.reshape(64, 8, D)
    second = second.reshape(64, 8, D)
    return jnp.concatenate([first, second], axis=1).astype(BF16).reshape(NZ, NX, NYL, 16, D)


def output_and_value_unit(blk):
    grad_output = mm(blk.mix_t[...].astype(BF16), blk.dy[...].astype(BF16))
    grad_value = mm_nt(blk.hid_t[...], blk.dpk_t[2 * D :, :])
    return pack_unit(grad_output, grad_value)


def query_and_key_unit(blk):
    hid_t = blk.hid_t[...]
    return pack_unit(mm_nt(hid_t, blk.dpk_t[0:D, :]), mm_nt(hid_t, blk.dpk_t[D : 2 * D, :]))


BLOCK_SCRATCH = (
    ("u", (CELLS, D), F32),
    ("normed", (CELLS, D), F32),
    ("spread", (CELLS, 128), F32),
    ("hid_t", (D, CELLS), BF16),
    ("pk", (CELLS, 3 * D), BF16),
    ("pk_t", (3 * D, CELLS), BF16),
    ("att", (HEADS, CELLS, CELLS), BF16),
    ("mix_t", (D, CELLS), F32),
    ("dy", (CELLS, D), F32),
    ("gm", (CELLS, D), BF16),
    ("gm_t", (D, CELLS), BF16),
    ("dpk_t", (3 * D, CELLS), BF16),
)


class Block:
    def __init__(self, refs):
        for (name, _, _), ref in zip(BLOCK_SCRATCH, refs):
            setattr(self, name, ref)


class Torus:
    def __init__(self):
        self.lat = lax.axis_index("lat")
        self.lon = lax.axis_index("lon")
        self.z = self.lat // 8
        self.x = (self.lat // 2) % 4
        self.y = (self.lon // 2) * 2 + self.lat % 2
        self.core = self.lon % 2

    def at(self, x=None, y=None, z=None, core=None):
        x = self.x if x is None else x
        y = self.y if y is None else y
        z = self.z if z is None else z
        core = self.core if core is None else core
        return (z * 8 + x * 2 + y % 2, (y // 2) * 2 + core)

    def shifted(self, dlat, dlon):
        return ((self.lat + dlat + 64) % 64, (self.lon + dlon + 4) % 4)

    def greeted(self):
        found = [self.shifted(*step) for step in ((1, 0), (-1, 0), (1, 1), (-1, -1), (0, 1), (0, -1))]
        found += [self.at(core=1 - self.core)]
        found += [self.in_plane(dx, dy) for dx, dy in PLANE]
        found += [self.in_column(dz, dh) for dz, dh in COLUMN]
        return found

    def in_plane(self, dx, dy):
        return self.at(x=(self.x + dx) % 4, y=(self.y + dy) % 4)

    def in_column(self, dz, dh):
        return self.at(z=(self.z + dz) % 8, y=(self.y + 2 * dh) % 4)


class Halo:
    STEPS = ((1, 0), (0, 1), (1, 1))

    def __init__(self, torus, index, sign, out_ref, in_ref, send_sem, recv_sem):
        self.out_ref = out_ref.at[index]
        self.in_ref = in_ref.at[index]
        self.copies = [
            pltpu.make_async_remote_copy(
                src_ref=out_ref.at[index, n],
                dst_ref=in_ref.at[index, n],
                send_sem=send_sem.at[index, n],
                recv_sem=recv_sem.at[index, n],
                device_id=torus.shifted(sign * step[0], sign * step[1]),
                device_id_type=MESH,
            )
            for n, step in enumerate(self.STEPS)
        ]

    def send(self, cells_ref):
        for n, copy in enumerate(self.copies):
            q = n + 1
            self.out_ref[n, 0:QUAD, :] = cells_ref[q * QUAD : q * QUAD + QUAD, :].astype(BF16)
            copy.start()

    def receive(self, cells_ref):
        for n, copy in enumerate(self.copies):
            q = n + 1
            copy.wait_recv()
            cells_ref[q * QUAD : q * QUAD + QUAD, :] = self.in_ref[n, 0:QUAD, :].astype(F32)

    def close(self):
        for copy in self.copies:
            copy.wait_send()


UNIT_SCRATCH = (
    ("whole", (NZ, NX, NYL, 16, D), BF16),
    ("core_in", (NZ, NX, NYL, 16, 256), BF16),
    ("half", (NZ, NX, NYL, 16, 256), BF16),
    ("last", (2, 2, 16, 128), F32),
)
PLANE_SCRATCH = UNIT_SCRATCH + (
    ("plane_in", (15, NZ, 16, 128), BF16),
    ("plane_sum", (NZ, 16, 128), BF16),
    ("column_in", (15, 16, 128), BF16),
)
Z_SCRATCH = UNIT_SCRATCH + (
    ("z_in", (7, NX, NYL, 16, 256), BF16),
    ("z_sum", (NX, NYL, 16, 256), BF16),
    ("plane_in", (15, 16, 256), BF16),
)
UNIT_SEMS = 32


class Unit:
    def __init__(self, torus, refs, send_sem, recv_sem):
        self.t = torus
        for (name, _, _), ref in zip(self.SCRATCH, refs):
            setattr(self, name, ref)
        self.send_sem, self.recv_sem = send_sem, recv_sem
        self.pending = []
        self.arriving = []

    def _copy(self, src, dst, sem, device):
        copy = pltpu.make_async_remote_copy(
            src_ref=src,
            dst_ref=dst,
            send_sem=self.send_sem.at[sem],
            recv_sem=self.recv_sem.at[sem],
            device_id=device,
            device_id_type=MESH,
        )
        copy.start()
        self.pending.append(copy)
        self.arriving.append(copy)

    def _arrived(self):
        for copy in self.arriving:
            copy.wait_recv()
        self.arriving = []

    def start(self):
        t = self.t
        cols = pl.ds(pl.multiple_of((1 - t.core) * 256, 256), 256)
        self._copy(self.whole.at[:, :, :, :, cols], self.core_in, 0, t.at(core=1 - t.core))

    def core_total(self):
        self._arrived()
        cols = pl.ds(pl.multiple_of(self.t.core * 256, 256), 256)
        self.half[...] = (self.whole[:, :, :, :, cols].astype(F32) + self.core_in[...].astype(F32)).astype(BF16)

    def send_last(self):
        t = self.t
        self._copy(self.last.at[t.core], self.last.at[t.core], 31, t.at(core=1 - t.core))

    def finish(self, first_ref, first_col, second_ref, second_col):
        self._arrived()
        for core in range(2):
            for high in range(2):
                off = core * 256 + high * 128
                first_ref[:, first_col + off : first_col + off + 128] = self.last[core, high, 0:8, :]
                second_ref[:, second_col + off : second_col + off + 128] = self.last[core, high, 8:16, :]

    def close(self):
        for copy in self.pending:
            copy.wait_send()


class PlaneUnit(Unit):
    SCRATCH = PLANE_SCRATCH

    def spread(self):
        t = self.t
        self.core_total()
        for dx, dy in PLANE:
            y = (t.y + dy) % 4
            cols = pl.ds(pl.multiple_of(y // 2 * 128, 128), 128)
            slot = (-dx) % 4 * 4 + (-dy) % 4 - 1
            self._copy(
                self.half.at[:, (t.x + dx) % 4, y % 2, :, cols], self.plane_in.at[slot], 1 + slot, t.in_plane(dx, dy)
            )

    def gather(self):
        t = self.t
        self._arrived()
        cols = pl.ds(pl.multiple_of(t.y // 2 * 128, 128), 128)
        total = self.half[:, t.x, t.y % 2, :, cols].astype(F32)
        for slot in range(15):
            total = total + self.plane_in[slot].astype(F32)
        self.plane_sum[...] = total.astype(BF16)
        for dz, dh in COLUMN:
            slot = (-dz) % 8 * 2 + dh - 1
            self._copy(self.plane_sum.at[(t.z + dz) % 8], self.column_in.at[slot], 16 + slot, t.in_column(dz, dh))

    def total(self):
        t = self.t
        self._arrived()
        mine = self.plane_sum[t.z].astype(F32)
        for dz in range(1, 8):
            mine = mine + self.column_in[dz * 2 - 1].astype(F32)
        other = self.column_in[0].astype(F32)
        for dz in range(1, 8):
            other = other + self.column_in[dz * 2].astype(F32)
        high = t.y // 2
        self.last[t.core, high] = mine
        self.last[t.core, 1 - high] = other
        self.send_last()


class ZUnit(Unit):
    SCRATCH = Z_SCRATCH

    def spread(self):
        t = self.t
        self.core_total()
        for dz in (4, 3, 5, 2, 6, 1, 7):
            self._copy(self.half.at[(t.z + dz) % 8], self.z_in.at[7 - dz], 8 - dz, t.in_column(dz, 0))

    def gather(self):
        t = self.t
        self._arrived()
        total = self.half[t.z].astype(F32)
        for slot in range(7):
            total = total + self.z_in[slot].astype(F32)
        self.z_sum[...] = total.astype(BF16)
        for dx, dy in PLANE:
            slot = (-dx) % 4 * 4 + (-dy) % 4 - 1
            self._copy(
                self.z_sum.at[(t.x + dx) % 4, (t.y + dy) % 2], self.plane_in.at[slot], 8 + slot, t.in_plane(dx, dy)
            )

    def total(self):
        t = self.t
        self._arrived()
        total = self.z_sum[t.x, t.y % 2].astype(F32)
        for slot in range(15):
            total = total + self.plane_in[slot].astype(F32)
        self.last[t.core, 0] = total[:, 0:128]
        self.last[t.core, 1] = total[:, 128:256]
        self.send_last()


UNIT_KINDS = (ZUnit, PlaneUnit, PlaneUnit, PlaneUnit)


def kernel(
    tokens_ref,
    land_ref,
    pole_ref,
    land_vec_ref,
    pole_vec_ref,
    w1_hbm,
    o1_hbm,
    w2_hbm,
    o2_hbm,
    cot_ref,
    layer_ref,
    tokens_grad_ref,
    ga1_ref,
    go1_ref,
    ga2_ref,
    go2_ref,
    *scratch,
):
    n = len(BLOCK_SCRATCH)
    one, two = Block(scratch[:n]), Block(scratch[n : 2 * n])
    rest = list(scratch[2 * n :])
    unit_refs = [[rest.pop(0) for _ in kind.SCRATCH] for kind in UNIT_KINDS]
    (w1_ref, o1_ref, w2_ref, o2_ref, cells_ref, mask_ref, halo_out, halo_in, load_sem, halo_send, halo_recv,
     red_send, red_recv) = rest

    torus = Torus()
    loads = [
        pltpu.make_async_copy(src, dst, load_sem.at[i])
        for i, (src, dst) in enumerate(((w1_hbm, w1_ref), (o1_hbm, o1_ref), (w2_hbm, w2_ref), (o2_hbm, o2_ref)))
    ]
    for load in loads:
        load.start()

    barrier = pltpu.get_barrier_semaphore()
    greeted = torus.greeted()
    for device in greeted:
        pl.semaphore_signal(barrier, inc=1, device_id=device, device_id_type=MESH)

    land = land_ref[...].astype(F32)
    at_cell = lax.broadcasted_iota(jnp.int32, (WLON, 1, WLON), 0)
    eye = at_cell == lax.broadcasted_iota(jnp.int32, (WLON, 1, WLON), 2)
    land_vec = land_vec_ref[...].astype(F32).reshape(1, 1, D)
    pole_vec = pole_vec_ref[...].astype(F32).reshape(1, 1, D)

    def mark(chunk, row, side):
        row_marks = jnp.broadcast_to(land[row : row + 1, :].reshape(1, 1, WLON), (WLON, 1, WLON))
        column = jnp.sum(jnp.where(eye, row_marks, 0.0), axis=2, keepdims=True)[side * 6 : side * 6 + 6]
        marked = chunk + column * land_vec + pole_ref[row].astype(F32) * pole_vec
        return marked.astype(BF16).astype(F32)

    field_to_cells(tokens_ref, one.u, mark)
    halos = [
        Halo(torus, i, sign, halo_out, halo_in, halo_send, halo_recv) for i, sign in enumerate((-1, -1, 1, 1))
    ]
    out2, query2, out1, query1 = (
        kind(torus, refs, red_send.at[i], red_recv.at[i]) for i, (kind, refs) in enumerate(zip(UNIT_KINDS, unit_refs))
    )

    loads[0].wait()
    loads[1].wait()
    first = forward(one, w1_ref, o1_ref, None)
    two.u[...] = first.astype(BF16).astype(F32)

    pl.semaphore_wait(barrier, len(greeted))
    halos[0].send(two.u)
    field_to_cells(cot_ref, two.dy)
    halos[1].send(two.dy)

    last = jnp.where(torus.lat == 63, 1.0, 0.0).astype(F32)
    far_k = (lax.broadcasted_iota(jnp.int32, (CELLS, CELLS), 0) // QUAD) % 2
    far_q = (lax.broadcasted_iota(jnp.int32, (CELLS, CELLS), 1) // QUAD) % 2
    mask_ref[...] = 1.0 - last * jnp.where(far_k == far_q, 0.0, 1.0)

    loads[2].wait()
    loads[3].wait()
    halos[0].receive(two.u)
    cells_ref[...] = forward(two, w2_ref, o2_ref, mask_ref)
    halos[2].send(cells_ref)
    halos[1].receive(two.dy)

    backward_values(two, o2_ref)
    backward_scores(two, range(HEADS))
    one.dy[...] = backward_input(two, w2_ref)
    halos[3].send(one.dy)
    out2.whole[...] = output_and_value_unit(two)
    out2.start()
    query2.whole[...] = query_and_key_unit(two)
    query2.start()
    out2.spread()
    query2.spread()

    halos[3].receive(one.dy)
    backward_values(one, o1_ref)
    out1.whole[...] = output_and_value_unit(one)
    out1.start()
    backward_scores(one, range(HEADS // 2))
    out1.spread()
    backward_scores(one, range(HEADS // 2, HEADS))
    query1.whole[...] = query_and_key_unit(one)
    query1.start()
    query1.spread()

    halos[2].receive(cells_ref)
    cells_to_field(cells_ref, layer_ref)
    cells_ref[...] = backward_input(one, w1_ref)
    cells_to_field(cells_ref, tokens_grad_ref)

    query2.gather()
    out1.gather()
    out2.gather()
    query1.gather()
    query2.total()
    out1.total()
    out2.total()
    query2.finish(ga2_ref, 0, ga2_ref, D)
    out2.finish(go2_ref, 0, ga2_ref, 2 * D)
    out1.finish(go1_ref, 0, ga1_ref, 2 * D)
    query1.total()
    query1.finish(ga1_ref, 0, ga1_ref, D)
    for each in halos + [out2, query2, out1, query1]:
        each.close()


def hand_over(*refs):
    for i in range(6):
        refs[6 + i][...] = refs[i][...]


def local(
    tokens,
    land_sea,
    pole_band,
    land_embedding,
    pole_embedding,
    attend_first,
    output_first,
    attend_second,
    output_second,
    cotangent,
):
    vmem = pl.BlockSpec(memory_space=pltpu.VMEM)
    smem = pl.BlockSpec(memory_space=pltpu.SMEM)
    hbm = pl.BlockSpec(memory_space=pl.ANY)
    field = jax.ShapeDtypeStruct((WLAT, WLON, LV, D), BF16)
    shapes = (
        field,
        field,
        jax.ShapeDtypeStruct((8, 3 * D), F32),
        jax.ShapeDtypeStruct((8, D), F32),
        jax.ShapeDtypeStruct((8, 3 * D), F32),
        jax.ShapeDtypeStruct((8, D), F32),
    )
    results = pl.pallas_call(
        kernel,
        out_shape=shapes,
        in_specs=[vmem, vmem, smem, vmem, vmem, hbm, hbm, hbm, hbm, vmem],
        out_specs=[vmem] * 6,
        scratch_shapes=[pltpu.VMEM(shape, dtype) for _, shape, dtype in BLOCK_SCRATCH * 2 + sum((k.SCRATCH for k in UNIT_KINDS), ())]
        + [
            pltpu.VMEM((D, 3 * D), BF16),
            pltpu.VMEM((D, D), BF16),
            pltpu.VMEM((D, 3 * D), BF16),
            pltpu.VMEM((D, D), BF16),
            pltpu.VMEM((CELLS, D), F32),
            pltpu.VMEM((CELLS, CELLS), F32),
            pltpu.VMEM((4, 3, SLAB, D), BF16),
            pltpu.VMEM((4, 3, SLAB, D), BF16),
            pltpu.SemaphoreType.DMA((4,)),
            pltpu.SemaphoreType.DMA((4, 3)),
            pltpu.SemaphoreType.DMA((4, 3)),
            pltpu.SemaphoreType.DMA((4, UNIT_SEMS)),
            pltpu.SemaphoreType.DMA((4, UNIT_SEMS)),
        ],
        compiler_params=pltpu.CompilerParams(
            collective_id=0, has_side_effects=True, vmem_limit_bytes=56 * 1024 * 1024
        ),
    )(
        tokens.transpose(1, 2, 0, 3),
        land_sea,
        pole_band,
        land_embedding,
        pole_embedding,
        attend_first,
        output_first,
        attend_second,
        output_second,
        cotangent.transpose(1, 2, 0, 3),
    )
    results = pl.pallas_call(
        hand_over,
        out_shape=shapes,
        in_specs=[vmem] * 6,
        out_specs=[vmem] * 6,
    )(*results)
    return tuple(r.transpose(2, 0, 1, 3) for r in results[:2]) + tuple(results[2:])


def solution(mesh):
    placed = (
        P(None, "lat", "lon", None),
        P("lat", "lon"),
        P("lat"),
        P(),
        P(),
        P(),
        P(),
        P(),
        P(),
        P(None, "lat", "lon", None),
    )
    return jax.shard_map(
        local,
        mesh=mesh,
        in_specs=placed,
        out_specs=(
            P(None, "lat", "lon", None),
            P(None, "lat", "lon", None),
            P("lat", None),
            P("lat", None),
            P("lat", None),
            P("lat", None),
        ),
        check_vma=False,
    )
```

```python
import functools
import math

import jax
import jax.numpy as jnp
from jax import lax
from jax.experimental import pallas as pl
from jax.experimental.pallas import tpu as pltpu
from jax.sharding import PartitionSpec as P

MESH = pl.DeviceIdType.MESH
BF16 = jnp.bfloat16
F32 = jnp.float32

D = 512
HEADS = 16
PER_HEAD = D // HEADS
LV = 2
WLAT = 6
WLON = 12
CELLS = LV * WLAT * WLON
QUAD = CELLS // 4
SLAB = 48
EPS = 1e-05
SCALE = 1.0 / math.sqrt(PER_HEAD)
EXP2_SCALE = SCALE * math.log2(math.e)

NZ, NX, NYL = 8, 4, 2
PLANE = [(dx, dy) for dx in (2, 1, 3, 0) for dy in (2, 1, 3, 0) if (dx, dy) != (0, 0)]
COLUMN = [(dz, dh) for dz in (4, 3, 5, 2, 6, 1, 7, 0) for dh in (1, 0) if (dz, dh) != (0, 0)]


def mm(left, right):
    return lax.dot_general(left, right, (((1,), (0,)), ((), ())), preferred_element_type=F32)


def mm_nt(left, right):
    return lax.dot_general(left, right, (((1,), (1,)), ((), ())), preferred_element_type=F32)


def chunk_offset(row, side):
    quadrant = (0 if row >= 3 else 1) + (0 if side == 1 else 2)
    return quadrant * QUAD + row % 3 * 12


def field_to_cells(field_ref, cells_ref, change=lambda chunk, row, side: chunk):
    for row in range(WLAT):
        for side in range(2):
            off = chunk_offset(row, side)
            chunk = field_ref[row, side * 6 : side * 6 + 6, :, :].astype(F32)
            cells_ref[off : off + 12, :] = change(chunk, row, side).reshape(12, D)


def cells_to_field(cells_ref, field_ref):
    for row in range(WLAT):
        for side in range(2):
            off = chunk_offset(row, side)
            field_ref[row, side * 6 : side * 6 + 6, :, :] = cells_ref[off : off + 12, :].reshape(6, LV, D).astype(BF16)


def layer_norm(u):
    centre = jnp.mean(u, axis=-1, keepdims=True)
    centred = u - centre
    spread = lax.rsqrt(jnp.mean(centred * centred, axis=-1, keepdims=True) + EPS)
    return centred * spread, spread


def head_lanes(head):
    lane = lax.broadcasted_iota(jnp.int32, (CELLS, 256), 1)
    return (lane // PER_HEAD) == (head % 8)


def head_rows(part, head):
    first = part * D + head * PER_HEAD
    return slice(first, first + PER_HEAD)


def forward(blk, w_ref, wo_ref, mask_ref):
    u = blk.u[...]
    normed, spread = layer_norm(u)
    blk.normed[...] = normed
    blk.spread[...] = jnp.broadcast_to(spread, (CELLS, 128))
    hidden = normed.astype(BF16)
    blk.hid_t[...] = hidden.T
    for part in range(3):
        cols = slice(part * D, part * D + D)
        packed = mm(hidden, w_ref[:, cols]).astype(BF16)
        blk.pk[:, cols] = packed
        blk.pk_t[cols, :] = packed.T

    def one_head(head):
        group = head // 8
        q_g = blk.pk[:, group * 256 : group * 256 + 256]
        k_g = blk.pk[:, D + group * 256 : D + group * 256 + 256]
        k_h = jnp.where(head_lanes(head), k_g, jnp.zeros_like(k_g))
        weights = jnp.exp2(mm_nt(k_h, q_g) * EXP2_SCALE)
        if mask_ref is not None:
            weights = weights * mask_ref[...]
        attention = (weights * (1.0 / jnp.sum(weights, axis=0, keepdims=True))).astype(BF16)
        blk.att[head] = attention

    for head in range(HEADS):
        one_head(head)
    for head in range(HEADS):
        blk.mix_t[head_rows(0, head), :] = mm(blk.pk_t[head_rows(2, head), :], blk.att[head])
    mixed = blk.mix_t[...].astype(BF16).T
    return u + mm(mixed, wo_ref[...])


def backward_mixed(blk, wo_ref):
    dy_low = blk.dy[...].astype(BF16)
    blk.gm[...] = mm_nt(dy_low, wo_ref[...]).astype(BF16)
    blk.gm_t[...] = blk.gm[...].T


def backward_values(blk):
    for head in range(HEADS):
        g_t = blk.gm_t[head_rows(0, head), :]
        blk.dpk_t[head_rows(2, head), :] = mm_nt(g_t, blk.att[head]).astype(BF16)


def backward_scores(blk, heads):
    for head in heads:
        group = head // 8
        v_g = blk.pk[:, 2 * D + group * 256 : 2 * D + group * 256 + 256]
        g_g = blk.gm[:, group * 256 : group * 256 + 256]
        v_h = jnp.where(head_lanes(head), v_g, jnp.zeros_like(v_g))
        grad_attention = mm_nt(v_h, g_g)
        rows = head_rows(0, head)
        inner = jnp.sum(blk.mix_t[rows, :] * blk.gm_t[rows, :].astype(F32), axis=0, keepdims=True)
        blk.dsc[head] = (blk.att[head].astype(F32) * (grad_attention - inner)).astype(BF16)
    for head in heads:
        rows, key_rows = head_rows(0, head), head_rows(1, head)
        grad_scores = blk.dsc[head]
        blk.dpk_t[rows, :] = (mm(blk.pk_t[key_rows, :], grad_scores) * SCALE).astype(BF16)
        blk.dpk_t[key_rows, :] = (mm_nt(blk.pk_t[rows, :], grad_scores) * SCALE).astype(BF16)


def backward_input(blk, w_ref):
    grad_hidden = mm(w_ref[...], blk.dpk_t[...]).T
    normed = blk.normed[...]
    spread = blk.spread[:, 0:1]
    return blk.dy[...] + spread * (
        grad_hidden
        - jnp.mean(grad_hidden, axis=-1, keepdims=True)
        - normed * jnp.mean(grad_hidden * normed, axis=-1, keepdims=True)
    )


def pack_unit(first, second):
    first = first.reshape(64, 8, D)
    second = second.reshape(64, 8, D)
    return jnp.concatenate([first, second], axis=1).astype(BF16).reshape(NZ, NX, NYL, 16, D)


def output_and_value_unit(blk):
    grad_output = mm(blk.mix_t[...].astype(BF16), blk.dy[...].astype(BF16))
    grad_value = mm_nt(blk.hid_t[...], blk.dpk_t[2 * D :, :])
    return pack_unit(grad_output, grad_value)


def query_and_key_unit(blk):
    hid_t = blk.hid_t[...]
    return pack_unit(mm_nt(hid_t, blk.dpk_t[0:D, :]), mm_nt(hid_t, blk.dpk_t[D : 2 * D, :]))


BLOCK_SCRATCH = (
    ("u", (CELLS, D), F32),
    ("normed", (CELLS, D), F32),
    ("spread", (CELLS, 128), F32),
    ("hid_t", (D, CELLS), BF16),
    ("pk", (CELLS, 3 * D), BF16),
    ("pk_t", (3 * D, CELLS), BF16),
    ("att", (HEADS, CELLS, CELLS), BF16),
    ("dsc", (HEADS, CELLS, CELLS), BF16),
    ("mix_t", (D, CELLS), F32),
    ("dy", (CELLS, D), F32),
    ("gm", (CELLS, D), BF16),
    ("gm_t", (D, CELLS), BF16),
    ("dpk_t", (3 * D, CELLS), BF16),
)


class Block:
    def __init__(self, refs):
        for (name, _, _), ref in zip(BLOCK_SCRATCH, refs):
            setattr(self, name, ref)


class Torus:
    def __init__(self):
        self.lat = lax.axis_index("lat")
        self.lon = lax.axis_index("lon")
        self.z = self.lat // 8
        self.x = (self.lat // 2) % 4
        self.y = (self.lon // 2) * 2 + self.lat % 2
        self.core = self.lon % 2

    def at(self, x=None, y=None, z=None, core=None):
        x = self.x if x is None else x
        y = self.y if y is None else y
        z = self.z if z is None else z
        core = self.core if core is None else core
        return (z * 8 + x * 2 + y % 2, (y // 2) * 2 + core)

    def shifted(self, dlat, dlon):
        return ((self.lat + dlat + 64) % 64, (self.lon + dlon + 4) % 4)

    def greeted(self):
        found = [self.shifted(*step) for step in ((1, 0), (-1, 0), (1, 1), (-1, -1), (0, 1), (0, -1))]
        found += [self.at(core=1 - self.core)]
        found += [self.in_plane(dx, dy) for dx, dy in PLANE]
        found += [self.in_column(dz, dh) for dz, dh in COLUMN]
        return found

    def in_plane(self, dx, dy):
        return self.at(x=(self.x + dx) % 4, y=(self.y + dy) % 4)

    def in_column(self, dz, dh):
        return self.at(z=(self.z + dz) % 8, y=(self.y + 2 * dh) % 4)


def wait_all(ref, sem):
    pltpu.make_async_copy(ref, ref, sem).wait()


class Halo:
    STEPS = ((1, 0), (0, 1), (1, 1))

    def __init__(self, torus, index, sign, out_ref, in_ref, send_sem, recv_sem):
        self.torus, self.sign = torus, sign
        self.out_ref, self.in_ref = out_ref.at[index], in_ref.at[index]
        self.send_sem, self.recv_sem = send_sem.at[index], recv_sem.at[index]

    def send(self, cells_ref):
        for n, (dlat, dlon) in enumerate(self.STEPS):
            q = n + 1
            self.out_ref[n, 0:QUAD, :] = cells_ref[q * QUAD : q * QUAD + QUAD, :].astype(BF16)
            pltpu.make_async_remote_copy(
                src_ref=self.out_ref.at[n],
                dst_ref=self.in_ref.at[n],
                send_sem=self.send_sem,
                recv_sem=self.recv_sem,
                device_id=self.torus.shifted(self.sign * dlat, self.sign * dlon),
                device_id_type=MESH,
            ).start()

    def receive(self, cells_ref):
        wait_all(self.in_ref, self.recv_sem)
        for n in range(3):
            q = n + 1
            cells_ref[q * QUAD : q * QUAD + QUAD, :] = self.in_ref[n, 0:QUAD, :].astype(F32)

    def close(self):
        wait_all(self.out_ref, self.send_sem)


UNIT_SCRATCH = (
    ("whole", (NZ, NX, NYL, 16, D), BF16),
    ("core_in", (NZ, NX, NYL, 16, 256), BF16),
    ("half", (NZ, NX, NYL, 16, 256), BF16),
    ("last", (2, 2, 16, 128), F32),
)
PLANE_SCRATCH = UNIT_SCRATCH + (
    ("plane_in", (15, NZ, 16, 128), BF16),
)
Z_SCRATCH = UNIT_SCRATCH + (
    ("z_in", (7, NX, NYL, 16, 256), BF16),
    ("z_sum", (NX, NYL, 16, 256), BF16),
    ("plane_in", (15, 16, 256), BF16),
)
UNIT_SEMS = 4
CORE, MIDDLE, PLANE_LATE, LAST = range(UNIT_SEMS)


class Unit:
    def __init__(self, torus, refs, send_sem, recv_sem):
        self.t = torus
        for (name, _, _), ref in zip(self.SCRATCH, refs):
            setattr(self, name, ref)
        self.send_sem, self.recv_sem = send_sem, recv_sem
        self.sent = []

    def _copy(self, src, dst, stage, device):
        pltpu.make_async_remote_copy(
            src_ref=src,
            dst_ref=dst,
            send_sem=self.send_sem.at[stage],
            recv_sem=self.recv_sem.at[stage],
            device_id=device,
            device_id_type=MESH,
        ).start()

    def _arrived(self, stage, ref):
        wait_all(ref, self.recv_sem.at[stage])
        self.sent.append((stage, ref))

    def start(self):
        t = self.t
        cols = pl.ds(pl.multiple_of((1 - t.core) * 256, 256), 256)
        self._copy(self.whole.at[:, :, :, :, cols], self.core_in, CORE, t.at(core=1 - t.core))

    def core_total(self):
        self._arrived(CORE, self.core_in)
        cols = pl.ds(pl.multiple_of(self.t.core * 256, 256), 256)
        self.half[...] = (self.whole[:, :, :, :, cols].astype(F32) + self.core_in[...].astype(F32)).astype(BF16)

    def send_last(self):
        t = self.t
        self._copy(self.last.at[t.core], self.last.at[t.core], LAST, t.at(core=1 - t.core))

    def finish(self, first_ref, first_col, second_ref, second_col):
        self._arrived(LAST, self.last.at[1 - self.t.core])
        for core in range(2):
            for high in range(2):
                off = core * 256 + high * 128
                first_ref[:, first_col + off : first_col + off + 128] = self.last[core, high, 0:8, :]
                second_ref[:, second_col + off : second_col + off + 128] = self.last[core, high, 8:16, :]

    def close(self):
        for stage, ref in self.sent:
            wait_all(ref, self.send_sem.at[stage])


class PlaneUnit(Unit):
    SCRATCH = PLANE_SCRATCH

    def spread(self):
        t = self.t
        self.core_total()
        for dx, dy in PLANE:
            y = (t.y + dy) % 4
            cols = pl.ds(pl.multiple_of(y // 2 * 128, 128), 128)
            slot = (-dx) % 4 * 4 + (-dy) % 4 - 1
            self._copy(
                self.half.at[:, (t.x + dx) % 4, y % 2, :, cols], self.plane_in.at[slot], MIDDLE, t.in_plane(dx, dy)
            )

    def plane_total(self, sum_ref, place):
        t = self.t
        self._arrived(MIDDLE, self.plane_in)
        cols = pl.ds(pl.multiple_of(t.y // 2 * 128, 128), 128)
        total = self.half[:, t.x, t.y % 2, :, cols].astype(F32)
        for slot in range(15):
            total = total + self.plane_in[slot].astype(F32)
        sum_ref[:, place] = total.astype(BF16)


class Column:
    def __init__(self, torus, units, sum_ref, in_ref, send_sem, recv_sem):
        self.t, self.units, self.sum, self.came = torus, units, sum_ref, in_ref
        self.send_sem, self.recv_sem = send_sem, recv_sem

    def send(self):
        t = self.t
        for dz, dh in COLUMN:
            slot = (-dz) % 8 * 2 + dh - 1
            pltpu.make_async_remote_copy(
                src_ref=self.sum.at[(t.z + dz) % 8],
                dst_ref=self.came.at[slot],
                send_sem=self.send_sem,
                recv_sem=self.recv_sem,
                device_id=t.in_column(dz, dh),
                device_id_type=MESH,
            ).start()

    def total(self):
        t = self.t
        wait_all(self.came, self.recv_sem)
        mine = self.sum[t.z].astype(F32)
        for dz in range(1, 8):
            mine = mine + self.came[dz * 2 - 1].astype(F32)
        other = self.came[0].astype(F32)
        for dz in range(1, 8):
            other = other + self.came[dz * 2].astype(F32)
        high = t.y // 2
        for place, unit in enumerate(self.units):
            unit.last[t.core, high] = mine[place]
            unit.last[t.core, 1 - high] = other[place]
            unit.send_last()

    def close(self):
        wait_all(self.came, self.send_sem)


class ZUnit(Unit):
    SCRATCH = Z_SCRATCH

    def spread(self):
        t = self.t
        self.core_total()
        for dz in (4, 3, 5, 2, 6, 1, 7):
            self._copy(self.half.at[(t.z + dz) % 8], self.z_in.at[7 - dz], MIDDLE, t.in_column(dz, 0))

    def gather(self):
        t = self.t
        self._arrived(MIDDLE, self.z_in)
        total = self.half[t.z].astype(F32)
        for slot in range(7):
            total = total + self.z_in[slot].astype(F32)
        self.z_sum[...] = total.astype(BF16)
        for dx, dy in PLANE:
            slot = (-dx) % 4 * 4 + (-dy) % 4 - 1
            self._copy(
                self.z_sum.at[(t.x + dx) % 4, (t.y + dy) % 2], self.plane_in.at[slot], PLANE_LATE, t.in_plane(dx, dy)
            )

    def total(self):
        t = self.t
        self._arrived(PLANE_LATE, self.plane_in)
        total = self.z_sum[t.x, t.y % 2].astype(F32)
        for slot in range(15):
            total = total + self.plane_in[slot].astype(F32)
        self.last[t.core, 0] = total[:, 0:128]
        self.last[t.core, 1] = total[:, 128:256]
        self.send_last()


UNIT_KINDS = (ZUnit, PlaneUnit, PlaneUnit, PlaneUnit)


def kernel(
    tokens_hbm,
    land_hbm,
    pole_ref,
    land_vec_hbm,
    pole_vec_hbm,
    w1_hbm,
    o1_hbm,
    w2_hbm,
    o2_hbm,
    cot_hbm,
    layer_ref,
    tokens_grad_ref,
    ga1_ref,
    go1_ref,
    ga2_ref,
    go2_ref,
    *scratch,
):
    n = len(BLOCK_SCRATCH)
    one, two = Block(scratch[:n]), Block(scratch[n : 2 * n])
    rest = list(scratch[2 * n :])
    unit_refs = [[rest.pop(0) for _ in kind.SCRATCH] for kind in UNIT_KINDS]
    (tokens_ref, cot_ref, land_ref, land_vec_ref, pole_vec_ref, w1_ref, o1_ref, w2_ref, o2_ref, cells_ref, mask_ref,
     sum2, sum1, came2, came1, halo_out, halo_in, load_sem, halo_send, halo_recv, red_send, red_recv, col_send,
     col_recv) = rest

    torus = Torus()
    loads = [
        pltpu.make_async_copy(src, dst, load_sem.at[i])
        for i, (src, dst) in enumerate(
            (
                (tokens_hbm, tokens_ref),
                (land_hbm, land_ref),
                (land_vec_hbm, land_vec_ref),
                (pole_vec_hbm, pole_vec_ref),
                (w1_hbm, w1_ref),
                (o1_hbm, o1_ref),
                (cot_hbm, cot_ref),
                (w2_hbm, w2_ref),
                (o2_hbm, o2_ref),
            )
        )
    ]
    for load in loads:
        load.start()

    barrier = pltpu.get_barrier_semaphore()
    greeted = torus.greeted()
    for device in greeted:
        pl.semaphore_signal(barrier, inc=1, device_id=device, device_id_type=MESH)

    for load in loads[:4]:
        load.wait()
    land = land_ref[...].astype(F32)
    at_cell = lax.broadcasted_iota(jnp.int32, (WLON, 1, WLON), 0)
    eye = at_cell == lax.broadcasted_iota(jnp.int32, (WLON, 1, WLON), 2)
    land_vec = land_vec_ref[...].astype(F32).reshape(1, 1, D)
    pole_vec = pole_vec_ref[...].astype(F32).reshape(1, 1, D)

    def mark(chunk, row, side):
        row_marks = jnp.broadcast_to(land[row : row + 1, :].reshape(1, 1, WLON), (WLON, 1, WLON))
        column = jnp.sum(jnp.where(eye, row_marks, 0.0), axis=2, keepdims=True)[side * 6 : side * 6 + 6]
        marked = chunk + column * land_vec + pole_ref[row].astype(F32) * pole_vec
        return marked.astype(BF16).astype(F32)

    field_to_cells(tokens_ref, one.u, mark)
    halos = [
        Halo(torus, i, sign, halo_out, halo_in, halo_send, halo_recv) for i, sign in enumerate((-1, -1, 1, 1))
    ]
    out2, query2, out1, query1 = (
        kind(torus, refs, red_send.at[i], red_recv.at[i]) for i, (kind, refs) in enumerate(zip(UNIT_KINDS, unit_refs))
    )
    column2 = Column(torus, [query2], sum2, came2, col_send.at[0], col_recv.at[0])
    column1 = Column(torus, [query1, out1], sum1, came1, col_send.at[1], col_recv.at[1])

    loads[4].wait()
    loads[5].wait()
    first = forward(one, w1_ref, o1_ref, None)
    two.u[...] = first.astype(BF16).astype(F32)

    pl.semaphore_wait(barrier, len(greeted))
    halos[0].send(two.u)
    loads[6].wait()
    field_to_cells(cot_ref, two.dy)
    halos[1].send(two.dy)

    last = jnp.where(torus.lat == 63, 1.0, 0.0).astype(F32)
    far_k = (lax.broadcasted_iota(jnp.int32, (CELLS, CELLS), 0) // QUAD) % 2
    far_q = (lax.broadcasted_iota(jnp.int32, (CELLS, CELLS), 1) // QUAD) % 2
    mask_ref[...] = 1.0 - last * jnp.where(far_k == far_q, 0.0, 1.0)

    loads[7].wait()
    loads[8].wait()
    halos[0].receive(two.u)
    cells_ref[...] = forward(two, w2_ref, o2_ref, mask_ref)
    halos[2].send(cells_ref)
    halos[1].receive(two.dy)

    backward_mixed(two, o2_ref)
    backward_values(two)
    backward_scores(two, range(HEADS))
    one.dy[...] = backward_input(two, w2_ref)
    halos[3].send(one.dy)
    out2.whole[...] = output_and_value_unit(two)
    out2.start()
    query2.whole[...] = query_and_key_unit(two)
    query2.start()
    out2.spread()
    query2.spread()

    halos[3].receive(one.dy)
    backward_mixed(one, o1_ref)
    backward_values(one)
    out1.whole[...] = output_and_value_unit(one)
    out1.start()
    backward_scores(one, range(HEADS))
    query1.whole[...] = query_and_key_unit(one)
    query1.start()
    out1.spread()
    query1.spread()

    halos[2].receive(cells_ref)
    cells_to_field(cells_ref, layer_ref)
    cells_ref[...] = backward_input(one, w1_ref)
    cells_to_field(cells_ref, tokens_grad_ref)

    query2.plane_total(sum2, 0)
    column2.send()
    out2.gather()
    out1.plane_total(sum1, 1)
    query1.plane_total(sum1, 0)
    column1.send()
    column2.total()
    out2.total()
    query2.finish(ga2_ref, 0, ga2_ref, D)
    out2.finish(go2_ref, 0, ga2_ref, 2 * D)
    column1.total()
    query1.finish(ga1_ref, 0, ga1_ref, D)
    out1.finish(go1_ref, 0, ga1_ref, 2 * D)
    for each in halos + [out2, query2, out1, query1, column2, column1]:
        each.close()


def hand_over(*refs):
    for i in range(6):
        refs[6 + i][...] = refs[i][...]


def local(
    tokens,
    land_sea,
    pole_band,
    land_embedding,
    pole_embedding,
    attend_first,
    output_first,
    attend_second,
    output_second,
    cotangent,
):
    vmem = pl.BlockSpec(memory_space=pltpu.VMEM)
    smem = pl.BlockSpec(memory_space=pltpu.SMEM)
    hbm = pl.BlockSpec(memory_space=pl.ANY)
    field = jax.ShapeDtypeStruct((WLAT, WLON, LV, D), BF16)
    shapes = (
        field,
        field,
        jax.ShapeDtypeStruct((8, 3 * D), F32),
        jax.ShapeDtypeStruct((8, D), F32),
        jax.ShapeDtypeStruct((8, 3 * D), F32),
        jax.ShapeDtypeStruct((8, D), F32),
    )
    results = pl.pallas_call(
        kernel,
        out_shape=shapes,
        in_specs=[hbm, hbm, smem, hbm, hbm, hbm, hbm, hbm, hbm, hbm],
        out_specs=[vmem] * 6,
        scratch_shapes=[pltpu.VMEM(shape, dtype) for _, shape, dtype in BLOCK_SCRATCH * 2 + sum((k.SCRATCH for k in UNIT_KINDS), ())]
        + [
            pltpu.VMEM((WLAT, WLON, LV, D), BF16),
            pltpu.VMEM((WLAT, WLON, LV, D), BF16),
            pltpu.VMEM((WLAT, WLON), jnp.int32),
            pltpu.VMEM((D,), BF16),
            pltpu.VMEM((D,), BF16),
            pltpu.VMEM((D, 3 * D), BF16),
            pltpu.VMEM((D, D), BF16),
            pltpu.VMEM((D, 3 * D), BF16),
            pltpu.VMEM((D, D), BF16),
            pltpu.VMEM((CELLS, D), F32),
            pltpu.VMEM((CELLS, CELLS), F32),
            pltpu.VMEM((NZ, 1, 16, 128), BF16),
            pltpu.VMEM((NZ, 2, 16, 128), BF16),
            pltpu.VMEM((15, 1, 16, 128), BF16),
            pltpu.VMEM((15, 2, 16, 128), BF16),
            pltpu.VMEM((4, 3, SLAB, D), BF16),
            pltpu.VMEM((4, 3, SLAB, D), BF16),
            pltpu.SemaphoreType.DMA((9,)),
            pltpu.SemaphoreType.DMA((4,)),
            pltpu.SemaphoreType.DMA((4,)),
            pltpu.SemaphoreType.DMA((4, UNIT_SEMS)),
            pltpu.SemaphoreType.DMA((4, UNIT_SEMS)),
            pltpu.SemaphoreType.DMA((2,)),
            pltpu.SemaphoreType.DMA((2,)),
        ],
        compiler_params=pltpu.CompilerParams(
            collective_id=0, has_side_effects=True, vmem_limit_bytes=56 * 1024 * 1024
        ),
    )(
        tokens.transpose(1, 2, 0, 3),
        land_sea,
        pole_band,
        land_embedding,
        pole_embedding,
        attend_first,
        output_first,
        attend_second,
        output_second,
        cotangent.transpose(1, 2, 0, 3),
    )
    results = pl.pallas_call(
        hand_over,
        out_shape=shapes,
        in_specs=[vmem] * 6,
        out_specs=[vmem] * 6,
    )(*results)
    return tuple(r.transpose(2, 0, 1, 3) for r in results[:2]) + tuple(results[2:])


def solution(mesh):
    placed = (
        P(None, "lat", "lon", None),
        P("lat", "lon"),
        P("lat"),
        P(),
        P(),
        P(),
        P(),
        P(),
        P(),
        P(None, "lat", "lon", None),
    )
    return jax.shard_map(
        local,
        mesh=mesh,
        in_specs=placed,
        out_specs=(
            P(None, "lat", "lon", None),
            P(None, "lat", "lon", None),
            P("lat", None),
            P("lat", None),
            P("lat", None),
            P("lat", None),
        ),
        check_vma=False,
    )
```

```python
import functools
import math

import jax
import jax.numpy as jnp
from jax import lax
from jax.experimental import pallas as pl
from jax.experimental.pallas import tpu as pltpu
from jax.sharding import PartitionSpec as P

MESH = pl.DeviceIdType.MESH
BF16 = jnp.bfloat16
F32 = jnp.float32

D = 512
HEADS = 16
PER_HEAD = D // HEADS
LV = 2
WLAT = 6
WLON = 12
CELLS = LV * WLAT * WLON
QUAD = CELLS // 4
SLAB = 48
EPS = 1e-05
SCALE = 1.0 / math.sqrt(PER_HEAD)
EXP2_SCALE = SCALE * math.log2(math.e)

NZ, NX, NYL = 8, 4, 2
COLUMN = [(dz, dh) for dz in (4, 3, 5, 2, 6, 1, 7, 0) for dh in (1, 0) if (dz, dh) != (0, 0)]


def mm(left, right):
    return lax.dot_general(left, right, (((1,), (0,)), ((), ())), preferred_element_type=F32)


def mm_nt(left, right):
    return lax.dot_general(left, right, (((1,), (1,)), ((), ())), preferred_element_type=F32)


def chunk_offset(row, side):
    quadrant = (0 if row >= 3 else 1) + (0 if side == 1 else 2)
    return quadrant * QUAD + row % 3 * 12


def field_to_cells(field_ref, cells_ref, change=lambda chunk, row, side: chunk):
    for row in range(WLAT):
        for side in range(2):
            off = chunk_offset(row, side)
            chunk = field_ref[row, side * 6 : side * 6 + 6, :, :].astype(F32)
            cells_ref[off : off + 12, :] = change(chunk, row, side).reshape(12, D)


def cells_to_field(cells_ref, field_ref):
    for row in range(WLAT):
        for side in range(2):
            off = chunk_offset(row, side)
            field_ref[row, side * 6 : side * 6 + 6, :, :] = cells_ref[off : off + 12, :].reshape(6, LV, D).astype(BF16)


def layer_norm(u):
    centre = jnp.mean(u, axis=-1, keepdims=True)
    centred = u - centre
    spread = lax.rsqrt(jnp.mean(centred * centred, axis=-1, keepdims=True) + EPS)
    return centred * spread, spread


def head_lanes(head):
    lane = lax.broadcasted_iota(jnp.int32, (CELLS, 256), 1)
    return (lane // PER_HEAD) == (head % 8)


def head_rows(part, head):
    first = part * D + head * PER_HEAD
    return slice(first, first + PER_HEAD)


def forward(blk, w_ref, wo_ref, mask_ref):
    u = blk.u[...]
    normed, spread = layer_norm(u)
    blk.normed[...] = normed
    blk.spread[...] = jnp.broadcast_to(spread, (CELLS, 128))
    hidden = normed.astype(BF16)
    blk.hid_t[...] = hidden.T
    for part in range(3):
        cols = slice(part * D, part * D + D)
        packed = mm(hidden, w_ref[:, cols]).astype(BF16)
        blk.pk[:, cols] = packed
        blk.pk_t[cols, :] = packed.T

    def one_head(head):
        group = head // 8
        q_g = blk.pk[:, group * 256 : group * 256 + 256]
        k_g = blk.pk[:, D + group * 256 : D + group * 256 + 256]
        k_h = jnp.where(head_lanes(head), k_g, jnp.zeros_like(k_g))
        weights = jnp.exp2(mm_nt(k_h, q_g) * EXP2_SCALE)
        if mask_ref is not None:
            weights = weights * mask_ref[...]
        attention = (weights * (1.0 / jnp.sum(weights, axis=0, keepdims=True))).astype(BF16)
        blk.att[head] = attention

    for head in range(HEADS):
        one_head(head)
    for head in range(HEADS):
        blk.mix_t[head_rows(0, head), :] = mm(blk.pk_t[head_rows(2, head), :], blk.att[head])
    mixed = blk.mix_t[...].astype(BF16).T
    return u + mm(mixed, wo_ref[...])


def backward_mixed(blk, wo_ref):
    dy_low = blk.dy[...].astype(BF16)
    blk.gm[...] = mm_nt(dy_low, wo_ref[...]).astype(BF16)
    blk.gm_t[...] = blk.gm[...].T


def backward_values(blk):
    for head in range(HEADS):
        g_t = blk.gm_t[head_rows(0, head), :]
        blk.dpk_t[head_rows(2, head), :] = mm_nt(g_t, blk.att[head]).astype(BF16)


def backward_scores(blk, heads):
    for head in heads:
        group = head // 8
        v_g = blk.pk[:, 2 * D + group * 256 : 2 * D + group * 256 + 256]
        g_g = blk.gm[:, group * 256 : group * 256 + 256]
        v_h = jnp.where(head_lanes(head), v_g, jnp.zeros_like(v_g))
        grad_attention = mm_nt(v_h, g_g)
        rows = head_rows(0, head)
        inner = jnp.sum(blk.mix_t[rows, :] * blk.gm_t[rows, :].astype(F32), axis=0, keepdims=True)
        blk.dsc[head] = (blk.att[head].astype(F32) * (grad_attention - inner)).astype(BF16)
    for head in heads:
        rows, key_rows = head_rows(0, head), head_rows(1, head)
        grad_scores = blk.dsc[head]
        blk.dpk_t[rows, :] = (mm(blk.pk_t[key_rows, :], grad_scores) * SCALE).astype(BF16)
        blk.dpk_t[key_rows, :] = (mm_nt(blk.pk_t[rows, :], grad_scores) * SCALE).astype(BF16)


def backward_input(blk, w_ref):
    grad_hidden = mm(w_ref[...], blk.dpk_t[...]).T
    normed = blk.normed[...]
    spread = blk.spread[:, 0:1]
    return blk.dy[...] + spread * (
        grad_hidden
        - jnp.mean(grad_hidden, axis=-1, keepdims=True)
        - normed * jnp.mean(grad_hidden * normed, axis=-1, keepdims=True)
    )


def pack_unit(first, second):
    first = first.reshape(64, 8, D)
    second = second.reshape(64, 8, D)
    return jnp.concatenate([first, second], axis=1).astype(BF16).reshape(NZ, NX, NYL, 16, D)


def output_and_value_unit(blk):
    grad_output = mm(blk.mix_t[...].astype(BF16), blk.dy[...].astype(BF16))
    grad_value = mm_nt(blk.hid_t[...], blk.dpk_t[2 * D :, :])
    return pack_unit(grad_output, grad_value)


def query_and_key_unit(blk):
    hid_t = blk.hid_t[...]
    return pack_unit(mm_nt(hid_t, blk.dpk_t[0:D, :]), mm_nt(hid_t, blk.dpk_t[D : 2 * D, :]))


BLOCK_SCRATCH = (
    ("u", (CELLS, D), F32),
    ("normed", (CELLS, D), F32),
    ("spread", (CELLS, 128), F32),
    ("hid_t", (D, CELLS), BF16),
    ("pk", (CELLS, 3 * D), BF16),
    ("pk_t", (3 * D, CELLS), BF16),
    ("att", (HEADS, CELLS, CELLS), BF16),
    ("dsc", (HEADS, CELLS, CELLS), BF16),
    ("mix_t", (D, CELLS), F32),
    ("dy", (CELLS, D), F32),
    ("gm", (CELLS, D), BF16),
    ("gm_t", (D, CELLS), BF16),
    ("dpk_t", (3 * D, CELLS), BF16),
)


class Block:
    def __init__(self, refs):
        for (name, _, _), ref in zip(BLOCK_SCRATCH, refs):
            setattr(self, name, ref)


class Torus:
    def __init__(self):
        self.lat = lax.axis_index("lat")
        self.lon = lax.axis_index("lon")
        self.z = self.lat // 8
        self.x = (self.lat // 2) % 4
        self.y = (self.lon // 2) * 2 + self.lat % 2
        self.core = self.lon % 2

    def at(self, x=None, y=None, z=None, core=None):
        x = self.x if x is None else x
        y = self.y if y is None else y
        z = self.z if z is None else z
        core = self.core if core is None else core
        return (z * 8 + x * 2 + y % 2, (y // 2) * 2 + core)

    def shifted(self, dlat, dlon):
        return ((self.lat + dlat + 64) % 64, (self.lon + dlon + 4) % 4)

    def greeted(self):
        found = [self.shifted(*step) for step in ((1, 0), (-1, 0), (1, 1), (-1, -1), (0, 1), (0, -1))]
        found += [self.at(core=1 - self.core)]
        found += [self.in_plane(*step) for step in ((2, 0), (0, 2), (1, 0), (3, 0), (0, 1), (0, 3))]
        found += [self.in_column(dz, dh) for dz, dh in COLUMN]
        return found

    def in_plane(self, dx, dy):
        return self.at(x=(self.x + dx) % 4, y=(self.y + dy) % 4)

    def in_column(self, dz, dh):
        return self.at(z=(self.z + dz) % 8, y=(self.y + 2 * dh) % 4)


def wait_all(ref, sem):
    pltpu.make_async_copy(ref, ref, sem).wait()


class Halo:
    STEPS = ((1, 0), (0, 1), (1, 1))

    def __init__(self, torus, index, sign, out_ref, in_ref, send_sem, recv_sem):
        self.torus, self.sign = torus, sign
        self.out_ref, self.in_ref = out_ref.at[index], in_ref.at[index]
        self.send_sem, self.recv_sem = send_sem.at[index], recv_sem.at[index]

    def send(self, cells_ref):
        for n, (dlat, dlon) in enumerate(self.STEPS):
            q = n + 1
            self.out_ref[n, 0:QUAD, :] = cells_ref[q * QUAD : q * QUAD + QUAD, :].astype(BF16)
            pltpu.make_async_remote_copy(
                src_ref=self.out_ref.at[n],
                dst_ref=self.in_ref.at[n],
                send_sem=self.send_sem,
                recv_sem=self.recv_sem,
                device_id=self.torus.shifted(self.sign * dlat, self.sign * dlon),
                device_id_type=MESH,
            ).start()

    def receive(self, cells_ref):
        wait_all(self.in_ref, self.recv_sem)
        for n in range(3):
            q = n + 1
            cells_ref[q * QUAD : q * QUAD + QUAD, :] = self.in_ref[n, 0:QUAD, :].astype(F32)

    def close(self):
        wait_all(self.out_ref, self.send_sem)


UNIT_SCRATCH = (
    ("whole", (NZ, NX, NYL, 16, D), BF16),
    ("core_in", (NZ, NX, NYL, 16, 256), BF16),
    ("half", (NZ, NX, NYL, 16, 256), BF16),
    ("last", (2, 2, 16, 128), F32),
)
STEP_SCRATCH = UNIT_SCRATCH + (
    ("x_in", (3, 4, NYL, 16, 256), BF16),
    ("x_sum", (4, NYL, 16, 256), BF16),
    ("y_in", (3, 4, NX, 16, 128), BF16),
    ("y_sum", (4, NX, 16, 128), BF16),
    ("xy_in", (3, 4, 16, 128), BF16),
    ("yx_in", (3, 4, 16, 128), BF16),
)
UNIT_SEMS = 6
CORE, X, Y, XY, YX, LAST = range(UNIT_SEMS)


class Unit:
    def __init__(self, torus, refs, send_sem, recv_sem):
        self.t = torus
        for (name, _, _), ref in zip(STEP_SCRATCH, refs):
            setattr(self, name, ref)
        self.send_sem, self.recv_sem = send_sem, recv_sem
        self.sent = []

    def _copy(self, src, dst, stage, device):
        pltpu.make_async_remote_copy(
            src_ref=src,
            dst_ref=dst,
            send_sem=self.send_sem.at[stage],
            recv_sem=self.recv_sem.at[stage],
            device_id=device,
            device_id_type=MESH,
        ).start()

    def _arrived(self, stage, ref):
        wait_all(ref, self.recv_sem.at[stage])
        self.sent.append((stage, ref))

    def start(self):
        t = self.t
        cols = pl.ds(pl.multiple_of((1 - t.core) * 256, 256), 256)
        self._copy(self.whole.at[:, :, :, :, cols], self.core_in, CORE, t.at(core=1 - t.core))

    def core_total(self):
        self._arrived(CORE, self.core_in)
        cols = pl.ds(pl.multiple_of(self.t.core * 256, 256), 256)
        self.half[...] = (self.whole[:, :, :, :, cols].astype(F32) + self.core_in[...].astype(F32)).astype(BF16)

    def send_last(self):
        t = self.t
        self._copy(self.last.at[t.core], self.last.at[t.core], LAST, t.at(core=1 - t.core))

    def finish(self, first_ref, first_col, second_ref, second_col):
        self._arrived(LAST, self.last.at[1 - self.t.core])
        for core in range(2):
            for high in range(2):
                off = core * 256 + high * 128
                first_ref[:, first_col + off : first_col + off + 128] = self.last[core, high, 0:8, :]
                second_ref[:, second_col + off : second_col + off + 128] = self.last[core, high, 8:16, :]

    def close(self):
        for stage, ref in self.sent:
            wait_all(ref, self.send_sem.at[stage])


    def _y_cols(self, dy=0):
        return pl.ds(pl.multiple_of((self.t.y + dy) % 4 // 2 * 128, 128), 128)

    def spread(self):
        t = self.t
        self.core_total()
        for d in (2, 1, 3):
            self._copy(self.half.at[0:4, (t.x + d) % 4], self.x_in.at[3 - d], X, t.in_plane(d, 0))
            self._copy(
                self.half.at[4:8, :, (t.y + d) % 2, :, self._y_cols(d)], self.y_in.at[3 - d], Y, t.in_plane(0, d)
            )

    def turn(self):
        t = self.t
        self._arrived(X, self.x_in)
        total = self.half[0:4, t.x].astype(F32)
        for slot in range(3):
            total = total + self.x_in[slot].astype(F32)
        self.x_sum[...] = total.astype(BF16)
        for d in (2, 1, 3):
            self._copy(self.x_sum.at[:, (t.y + d) % 2, :, self._y_cols(d)], self.xy_in.at[3 - d], XY, t.in_plane(0, d))
        self._arrived(Y, self.y_in)
        total = self.half[4:8, :, t.y % 2, :, self._y_cols()].astype(F32)
        for slot in range(3):
            total = total + self.y_in[slot].astype(F32)
        self.y_sum[...] = total.astype(BF16)
        for d in (2, 1, 3):
            self._copy(self.y_sum.at[:, (t.x + d) % 4], self.yx_in.at[3 - d], YX, t.in_plane(d, 0))

    def plane_total(self, sum_ref, place):
        t = self.t
        self._arrived(XY, self.xy_in)
        total = self.x_sum[:, t.y % 2, :, self._y_cols()].astype(F32)
        for slot in range(3):
            total = total + self.xy_in[slot].astype(F32)
        sum_ref[0:4, place] = total.astype(BF16)
        self._arrived(YX, self.yx_in)
        total = self.y_sum[:, t.x].astype(F32)
        for slot in range(3):
            total = total + self.yx_in[slot].astype(F32)
        sum_ref[4:8, place] = total.astype(BF16)


class Column:
    def __init__(self, torus, units, sum_ref, in_ref, send_sem, recv_sem):
        self.t, self.units, self.sum, self.came = torus, units, sum_ref, in_ref
        self.send_sem, self.recv_sem = send_sem, recv_sem

    def send(self):
        t = self.t
        for dz, dh in COLUMN:
            slot = (-dz) % 8 * 2 + dh - 1
            pltpu.make_async_remote_copy(
                src_ref=self.sum.at[(t.z + dz) % 8],
                dst_ref=self.came.at[slot],
                send_sem=self.send_sem,
                recv_sem=self.recv_sem,
                device_id=t.in_column(dz, dh),
                device_id_type=MESH,
            ).start()

    def total(self):
        t = self.t
        wait_all(self.came, self.recv_sem)
        mine = self.sum[t.z].astype(F32)
        for dz in range(1, 8):
            mine = mine + self.came[dz * 2 - 1].astype(F32)
        other = self.came[0].astype(F32)
        for dz in range(1, 8):
            other = other + self.came[dz * 2].astype(F32)
        high = t.y // 2
        for place, unit in enumerate(self.units):
            unit.last[t.core, high] = mine[place]
            unit.last[t.core, 1 - high] = other[place]
            unit.send_last()

    def close(self):
        wait_all(self.came, self.send_sem)


def kernel(
    tokens_hbm,
    land_hbm,
    pole_ref,
    land_vec_hbm,
    pole_vec_hbm,
    w1_hbm,
    o1_hbm,
    w2_hbm,
    o2_hbm,
    cot_hbm,
    layer_ref,
    tokens_grad_ref,
    ga1_ref,
    go1_ref,
    ga2_ref,
    go2_ref,
    *scratch,
):
    n = len(BLOCK_SCRATCH)
    one, two = Block(scratch[:n]), Block(scratch[n : 2 * n])
    rest = list(scratch[2 * n :])
    unit_refs = [[rest.pop(0) for _ in STEP_SCRATCH] for _ in range(4)]
    (tokens_ref, cot_ref, land_ref, land_vec_ref, pole_vec_ref, w1_ref, o1_ref, w2_ref, o2_ref, cells_ref, mask_ref,
     sum2, sum1, came2, came1, halo_out, halo_in, load_sem, halo_send, halo_recv, red_send, red_recv, col_send,
     col_recv) = rest

    torus = Torus()
    loads = [
        pltpu.make_async_copy(src, dst, load_sem.at[i])
        for i, (src, dst) in enumerate(
            (
                (tokens_hbm, tokens_ref),
                (land_hbm, land_ref),
                (land_vec_hbm, land_vec_ref),
                (pole_vec_hbm, pole_vec_ref),
                (w1_hbm, w1_ref),
                (o1_hbm, o1_ref),
                (cot_hbm, cot_ref),
                (w2_hbm, w2_ref),
                (o2_hbm, o2_ref),
            )
        )
    ]
    for load in loads:
        load.start()

    barrier = pltpu.get_barrier_semaphore()
    greeted = torus.greeted()
    for device in greeted:
        pl.semaphore_signal(barrier, inc=1, device_id=device, device_id_type=MESH)

    for load in loads[:4]:
        load.wait()
    land = land_ref[...].astype(F32)
    at_cell = lax.broadcasted_iota(jnp.int32, (WLON, 1, WLON), 0)
    eye = at_cell == lax.broadcasted_iota(jnp.int32, (WLON, 1, WLON), 2)
    land_vec = land_vec_ref[...].astype(F32).reshape(1, 1, D)
    pole_vec = pole_vec_ref[...].astype(F32).reshape(1, 1, D)

    def mark(chunk, row, side):
        row_marks = jnp.broadcast_to(land[row : row + 1, :].reshape(1, 1, WLON), (WLON, 1, WLON))
        column = jnp.sum(jnp.where(eye, row_marks, 0.0), axis=2, keepdims=True)[side * 6 : side * 6 + 6]
        marked = chunk + column * land_vec + pole_ref[row].astype(F32) * pole_vec
        return marked.astype(BF16).astype(F32)

    field_to_cells(tokens_ref, one.u, mark)
    halos = [
        Halo(torus, i, sign, halo_out, halo_in, halo_send, halo_recv) for i, sign in enumerate((-1, -1, 1, 1))
    ]
    out2, query2, out1, query1 = (
        Unit(torus, refs, red_send.at[i], red_recv.at[i]) for i, refs in enumerate(unit_refs)
    )
    column2 = Column(torus, [query2, out2], sum2, came2, col_send.at[0], col_recv.at[0])
    column1 = Column(torus, [query1, out1], sum1, came1, col_send.at[1], col_recv.at[1])

    loads[4].wait()
    loads[5].wait()
    first = forward(one, w1_ref, o1_ref, None)
    two.u[...] = first.astype(BF16).astype(F32)

    pl.semaphore_wait(barrier, len(greeted))
    halos[0].send(two.u)
    loads[6].wait()
    field_to_cells(cot_ref, two.dy)
    halos[1].send(two.dy)

    last = jnp.where(torus.lat == 63, 1.0, 0.0).astype(F32)
    far_k = (lax.broadcasted_iota(jnp.int32, (CELLS, CELLS), 0) // QUAD) % 2
    far_q = (lax.broadcasted_iota(jnp.int32, (CELLS, CELLS), 1) // QUAD) % 2
    mask_ref[...] = 1.0 - last * jnp.where(far_k == far_q, 0.0, 1.0)

    loads[7].wait()
    loads[8].wait()
    halos[0].receive(two.u)
    cells_ref[...] = forward(two, w2_ref, o2_ref, mask_ref)
    halos[2].send(cells_ref)
    halos[1].receive(two.dy)

    backward_mixed(two, o2_ref)
    backward_values(two)
    backward_scores(two, range(HEADS))
    one.dy[...] = backward_input(two, w2_ref)
    halos[3].send(one.dy)
    out2.whole[...] = output_and_value_unit(two)
    out2.start()
    query2.whole[...] = query_and_key_unit(two)
    query2.start()
    out2.spread()
    query2.spread()

    halos[3].receive(one.dy)
    backward_mixed(one, o1_ref)
    backward_scores(one, range(HEADS))
    query1.whole[...] = query_and_key_unit(one)
    query1.start()
    backward_values(one)
    out1.whole[...] = output_and_value_unit(one)
    out1.start()
    query1.spread()
    out1.spread()

    halos[2].receive(cells_ref)
    cells_to_field(cells_ref, layer_ref)
    cells_ref[...] = backward_input(one, w1_ref)
    cells_to_field(cells_ref, tokens_grad_ref)
    out2.turn()
    query2.turn()

    query1.turn()
    out1.turn()
    out2.plane_total(sum2, 1)
    query2.plane_total(sum2, 0)
    column2.send()
    query1.plane_total(sum1, 0)
    out1.plane_total(sum1, 1)
    column1.send()
    column2.total()
    query2.finish(ga2_ref, 0, ga2_ref, D)
    out2.finish(go2_ref, 0, ga2_ref, 2 * D)
    column1.total()
    query1.finish(ga1_ref, 0, ga1_ref, D)
    out1.finish(go1_ref, 0, ga1_ref, 2 * D)
    for each in halos + [out2, query2, out1, query1, column2, column1]:
        each.close()


def hand_over(*refs):
    for i in range(6):
        refs[6 + i][...] = refs[i][...]


def local(
    tokens,
    land_sea,
    pole_band,
    land_embedding,
    pole_embedding,
    attend_first,
    output_first,
    attend_second,
    output_second,
    cotangent,
):
    vmem = pl.BlockSpec(memory_space=pltpu.VMEM)
    smem = pl.BlockSpec(memory_space=pltpu.SMEM)
    hbm = pl.BlockSpec(memory_space=pl.ANY)
    field = jax.ShapeDtypeStruct((WLAT, WLON, LV, D), BF16)
    shapes = (
        field,
        field,
        jax.ShapeDtypeStruct((8, 3 * D), F32),
        jax.ShapeDtypeStruct((8, D), F32),
        jax.ShapeDtypeStruct((8, 3 * D), F32),
        jax.ShapeDtypeStruct((8, D), F32),
    )
    results = pl.pallas_call(
        kernel,
        out_shape=shapes,
        in_specs=[hbm, hbm, smem, hbm, hbm, hbm, hbm, hbm, hbm, hbm],
        out_specs=[vmem] * 6,
        scratch_shapes=[pltpu.VMEM(shape, dtype) for _, shape, dtype in BLOCK_SCRATCH * 2 + STEP_SCRATCH * 4]
        + [
            pltpu.VMEM((WLAT, WLON, LV, D), BF16),
            pltpu.VMEM((WLAT, WLON, LV, D), BF16),
            pltpu.VMEM((WLAT, WLON), jnp.int32),
            pltpu.VMEM((D,), BF16),
            pltpu.VMEM((D,), BF16),
            pltpu.VMEM((D, 3 * D), BF16),
            pltpu.VMEM((D, D), BF16),
            pltpu.VMEM((D, 3 * D), BF16),
            pltpu.VMEM((D, D), BF16),
            pltpu.VMEM((CELLS, D), F32),
            pltpu.VMEM((CELLS, CELLS), F32),
            pltpu.VMEM((NZ, 2, 16, 128), BF16),
            pltpu.VMEM((NZ, 2, 16, 128), BF16),
            pltpu.VMEM((15, 2, 16, 128), BF16),
            pltpu.VMEM((15, 2, 16, 128), BF16),
            pltpu.VMEM((4, 3, SLAB, D), BF16),
            pltpu.VMEM((4, 3, SLAB, D), BF16),
            pltpu.SemaphoreType.DMA((9,)),
            pltpu.SemaphoreType.DMA((4,)),
            pltpu.SemaphoreType.DMA((4,)),
            pltpu.SemaphoreType.DMA((4, UNIT_SEMS)),
            pltpu.SemaphoreType.DMA((4, UNIT_SEMS)),
            pltpu.SemaphoreType.DMA((2,)),
            pltpu.SemaphoreType.DMA((2,)),
        ],
        compiler_params=pltpu.CompilerParams(
            collective_id=0, has_side_effects=True, vmem_limit_bytes=56 * 1024 * 1024
        ),
    )(
        tokens.transpose(1, 2, 0, 3),
        land_sea,
        pole_band,
        land_embedding,
        pole_embedding,
        attend_first,
        output_first,
        attend_second,
        output_second,
        cotangent.transpose(1, 2, 0, 3),
    )
    results = pl.pallas_call(
        hand_over,
        out_shape=shapes,
        in_specs=[vmem] * 6,
        out_specs=[vmem] * 6,
    )(*results)
    return tuple(r.transpose(2, 0, 1, 3) for r in results[:2]) + tuple(results[2:])


def solution(mesh):
    placed = (
        P(None, "lat", "lon", None),
        P("lat", "lon"),
        P("lat"),
        P(),
        P(),
        P(),
        P(),
        P(),
        P(),
        P(None, "lat", "lon", None),
    )
    return jax.shard_map(
        local,
        mesh=mesh,
        in_specs=placed,
        out_specs=(
            P(None, "lat", "lon", None),
            P(None, "lat", "lon", None),
            P("lat", None),
            P("lat", None),
            P("lat", None),
            P("lat", None),
        ),
        check_vma=False,
    )
```

```python
import functools
import math

import jax
import jax.numpy as jnp
from jax import lax
from jax.experimental import pallas as pl
from jax.experimental.pallas import tpu as pltpu
from jax.sharding import PartitionSpec as P

MESH = pl.DeviceIdType.MESH
BF16 = jnp.bfloat16
F32 = jnp.float32

D = 512
HEADS = 16
PER_HEAD = D // HEADS
LV = 2
WLAT = 6
WLON = 12
CELLS = LV * WLAT * WLON
QUAD = CELLS // 4
SLAB = 48
EPS = 1e-05
SCALE = 1.0 / math.sqrt(PER_HEAD)
EXP2_SCALE = SCALE * math.log2(math.e)

NZ, NX, NYL = 8, 4, 2
COLUMN = [(dz, dh) for dz in (4, 3, 5, 2, 6, 1, 7, 0) for dh in (1, 0) if (dz, dh) != (0, 0)]


def mm(left, right):
    return lax.dot_general(left, right, (((1,), (0,)), ((), ())), preferred_element_type=F32)


def mm_nt(left, right):
    return lax.dot_general(left, right, (((1,), (1,)), ((), ())), preferred_element_type=F32)


def chunk_offset(row, side):
    quadrant = (0 if row >= 3 else 1) + (0 if side == 1 else 2)
    return quadrant * QUAD + row % 3 * 12


def field_to_cells(field_ref, cells_ref, change=lambda chunk, row, side: chunk):
    for row in range(WLAT):
        for side in range(2):
            off = chunk_offset(row, side)
            chunk = field_ref[row, side * 6 : side * 6 + 6, :, :].astype(F32)
            cells_ref[off : off + 12, :] = change(chunk, row, side).reshape(12, D)


def cells_to_field(cells_ref, field_ref):
    for row in range(WLAT):
        for side in range(2):
            off = chunk_offset(row, side)
            field_ref[row, side * 6 : side * 6 + 6, :, :] = cells_ref[off : off + 12, :].reshape(6, LV, D).astype(BF16)


def layer_norm(u):
    centre = jnp.mean(u, axis=-1, keepdims=True)
    centred = u - centre
    spread = lax.rsqrt(jnp.mean(centred * centred, axis=-1, keepdims=True) + EPS)
    return centred * spread, spread


def head_lanes(head):
    lane = lax.broadcasted_iota(jnp.int32, (CELLS, 256), 1)
    return (lane // PER_HEAD) == (head % 8)


def head_rows(part, head):
    first = part * D + head * PER_HEAD
    return slice(first, first + PER_HEAD)


def forward(blk, w_ref, wo_ref, mask_ref):
    u = blk.u[...]
    normed, spread = layer_norm(u)
    blk.normed[...] = normed
    blk.spread[...] = jnp.broadcast_to(spread, (CELLS, 128))
    hidden = normed.astype(BF16)
    blk.hid_t[...] = hidden.T
    for part in range(3):
        cols = slice(part * D, part * D + D)
        packed = mm(hidden, w_ref[:, cols]).astype(BF16)
        blk.pk[:, cols] = packed
        blk.pk_t[cols, :] = packed.T

    def one_head(head):
        group = head // 8
        q_g = blk.pk[:, group * 256 : group * 256 + 256]
        k_g = blk.pk[:, D + group * 256 : D + group * 256 + 256]
        k_h = jnp.where(head_lanes(head), k_g, jnp.zeros_like(k_g))
        weights = jnp.exp2(mm_nt(k_h, q_g) * EXP2_SCALE)
        if mask_ref is not None:
            weights = weights * mask_ref[...]
        attention = (weights * (1.0 / jnp.sum(weights, axis=0, keepdims=True))).astype(BF16)
        blk.att[head] = attention

    for head in range(HEADS):
        one_head(head)
    for head in range(HEADS):
        blk.mix_t[head_rows(0, head), :] = mm(blk.pk_t[head_rows(2, head), :], blk.att[head])
    mixed = blk.mix_t[...].astype(BF16).T
    return u + mm(mixed, wo_ref[...])


def backward_mixed(blk, wo_ref):
    dy_low = blk.dy[...].astype(BF16)
    blk.gm[...] = mm_nt(dy_low, wo_ref[...]).astype(BF16)
    blk.gm_t[...] = blk.gm[...].T


def backward_values(blk):
    for head in range(HEADS):
        g_t = blk.gm_t[head_rows(0, head), :]
        blk.dpk_t[head_rows(2, head), :] = mm_nt(g_t, blk.att[head]).astype(BF16)


def backward_scores(blk, heads):
    for head in heads:
        group = head // 8
        v_g = blk.pk[:, 2 * D + group * 256 : 2 * D + group * 256 + 256]
        g_g = blk.gm[:, group * 256 : group * 256 + 256]
        v_h = jnp.where(head_lanes(head), v_g, jnp.zeros_like(v_g))
        grad_attention = mm_nt(v_h, g_g)
        rows = head_rows(0, head)
        inner = jnp.sum(blk.mix_t[rows, :] * blk.gm_t[rows, :].astype(F32), axis=0, keepdims=True)
        blk.dsc[head] = (blk.att[head].astype(F32) * (grad_attention - inner)).astype(BF16)
    for head in heads:
        rows, key_rows = head_rows(0, head), head_rows(1, head)
        grad_scores = blk.dsc[head]
        blk.dpk_t[rows, :] = (mm(blk.pk_t[key_rows, :], grad_scores) * SCALE).astype(BF16)
        blk.dpk_t[key_rows, :] = (mm_nt(blk.pk_t[rows, :], grad_scores) * SCALE).astype(BF16)


def backward_input(blk, w_ref):
    grad_hidden = mm(w_ref[...], blk.dpk_t[...]).T
    normed = blk.normed[...]
    spread = blk.spread[:, 0:1]
    return blk.dy[...] + spread * (
        grad_hidden
        - jnp.mean(grad_hidden, axis=-1, keepdims=True)
        - normed * jnp.mean(grad_hidden * normed, axis=-1, keepdims=True)
    )


def pack_unit(first, second):
    first = first.reshape(64, 8, D)
    second = second.reshape(64, 8, D)
    return jnp.concatenate([first, second], axis=1).astype(BF16).reshape(NZ, NX, NYL, 16, D)


def output_and_value_unit(blk):
    grad_output = mm(blk.mix_t[...].astype(BF16), blk.dy[...].astype(BF16))
    grad_value = mm_nt(blk.hid_t[...], blk.dpk_t[2 * D :, :])
    return pack_unit(grad_output, grad_value)


def query_and_key_unit(blk):
    hid_t = blk.hid_t[...]
    return pack_unit(mm_nt(hid_t, blk.dpk_t[0:D, :]), mm_nt(hid_t, blk.dpk_t[D : 2 * D, :]))


BLOCK_SCRATCH = (
    ("u", (CELLS, D), F32),
    ("normed", (CELLS, D), F32),
    ("spread", (CELLS, 128), F32),
    ("hid_t", (D, CELLS), BF16),
    ("pk", (CELLS, 3 * D), BF16),
    ("pk_t", (3 * D, CELLS), BF16),
    ("att", (HEADS, CELLS, CELLS), BF16),
    ("dsc", (HEADS, CELLS, CELLS), BF16),
    ("mix_t", (D, CELLS), F32),
    ("dy", (CELLS, D), F32),
    ("gm", (CELLS, D), BF16),
    ("gm_t", (D, CELLS), BF16),
    ("dpk_t", (3 * D, CELLS), BF16),
)


class Block:
    def __init__(self, refs):
        for (name, _, _), ref in zip(BLOCK_SCRATCH, refs):
            setattr(self, name, ref)


class Torus:
    def __init__(self):
        self.lat = lax.axis_index("lat")
        self.lon = lax.axis_index("lon")
        self.z = self.lat // 8
        self.x = (self.lat // 2) % 4
        self.y = (self.lon // 2) * 2 + self.lat % 2
        self.core = self.lon % 2

    def at(self, x=None, y=None, z=None, core=None):
        x = self.x if x is None else x
        y = self.y if y is None else y
        z = self.z if z is None else z
        core = self.core if core is None else core
        return (z * 8 + x * 2 + y % 2, (y // 2) * 2 + core)

    def shifted(self, dlat, dlon):
        return ((self.lat + dlat + 64) % 64, (self.lon + dlon + 4) % 4)

    def greeted(self):
        found = [self.shifted(*step) for step in ((1, 0), (-1, 0), (1, 1), (-1, -1), (0, 1), (0, -1))]
        found += [self.at(core=1 - self.core)]
        found += [self.in_plane(*step) for step in ((2, 0), (0, 2), (1, 0), (3, 0), (0, 1), (0, 3))]
        found += [self.in_column(dz, dh) for dz, dh in COLUMN]
        return found

    def in_plane(self, dx, dy):
        return self.at(x=(self.x + dx) % 4, y=(self.y + dy) % 4)

    def in_column(self, dz, dh):
        return self.at(z=(self.z + dz) % 8, y=(self.y + 2 * dh) % 4)


def wait_all(ref, sem):
    pltpu.make_async_copy(ref, ref, sem).wait()


class Halo:
    STEPS = ((1, 0), (0, 1), (1, 1))

    def __init__(self, torus, index, sign, out_ref, in_ref, send_sem, recv_sem):
        self.torus, self.sign = torus, sign
        self.out_ref, self.in_ref = out_ref.at[index], in_ref.at[index]
        self.send_sem, self.recv_sem = send_sem.at[index], recv_sem.at[index]

    def send(self, cells_ref):
        for n, (dlat, dlon) in enumerate(self.STEPS):
            q = n + 1
            self.out_ref[n, 0:QUAD, :] = cells_ref[q * QUAD : q * QUAD + QUAD, :].astype(BF16)
            pltpu.make_async_remote_copy(
                src_ref=self.out_ref.at[n],
                dst_ref=self.in_ref.at[n],
                send_sem=self.send_sem,
                recv_sem=self.recv_sem,
                device_id=self.torus.shifted(self.sign * dlat, self.sign * dlon),
                device_id_type=MESH,
            ).start()

    def receive(self, cells_ref):
        wait_all(self.in_ref, self.recv_sem)
        for n in range(3):
            q = n + 1
            cells_ref[q * QUAD : q * QUAD + QUAD, :] = self.in_ref[n, 0:QUAD, :].astype(F32)

    def close(self):
        wait_all(self.out_ref, self.send_sem)


def group_scratch(n):
    return (
        ("whole", (n, NZ, NX, NYL, 16, D), BF16),
        ("core_in", (n, NZ, NX, NYL, 16, 256), BF16),
        ("half", (n, NZ, NX, NYL, 16, 256), BF16),
        ("x_in", (3, n, 4, NYL, 16, 256), BF16),
        ("x_sum", (n, 4, NYL, 16, 256), BF16),
        ("y_in", (3, n, 4, NX, 16, 128), BF16),
        ("y_sum", (n, 4, NX, 16, 128), BF16),
        ("xy_in", (3, n, 4, 16, 128), BF16),
        ("yx_in", (3, n, 4, 16, 128), BF16),
        ("last", (2, 2, n, 16, 128), F32),
    )


GROUPS = (2, 2)
UNIT_SEMS = 6
CORE, X, Y, XY, YX, LAST = range(UNIT_SEMS)


class Group:
    def __init__(self, torus, n, refs, send_sem, recv_sem):
        self.t, self.n = torus, n
        for (name, _, _), ref in zip(group_scratch(n), refs):
            setattr(self, name, ref)
        self.send_sem, self.recv_sem = send_sem, recv_sem
        self.sent = []

    def _copy(self, src, dst, stage, device):
        pltpu.make_async_remote_copy(
            src_ref=src,
            dst_ref=dst,
            send_sem=self.send_sem.at[stage],
            recv_sem=self.recv_sem.at[stage],
            device_id=device,
            device_id_type=MESH,
        ).start()

    def _arrived(self, stage, ref):
        wait_all(ref, self.recv_sem.at[stage])
        self.sent.append((stage, ref))

    def start(self, unit, gradients):
        t = self.t
        self.whole[unit] = gradients
        cols = pl.ds(pl.multiple_of((1 - t.core) * 256, 256), 256)
        self._copy(self.whole.at[unit, :, :, :, :, cols], self.core_in.at[unit], CORE, t.at(core=1 - t.core))

    def core_total(self):
        self._arrived(CORE, self.core_in)
        cols = pl.ds(pl.multiple_of(self.t.core * 256, 256), 256)
        self.half[...] = self.whole[:, :, :, :, :, cols] + self.core_in[...]

    def send_last(self):
        t = self.t
        self._copy(self.last.at[t.core], self.last.at[t.core], LAST, t.at(core=1 - t.core))

    def finish(self, unit, first_ref, first_col, second_ref, second_col):
        if unit == 0:
            self._arrived(LAST, self.last.at[1 - self.t.core])
        for core in range(2):
            for high in range(2):
                off = core * 256 + high * 128
                first_ref[:, first_col + off : first_col + off + 128] = self.last[core, high, unit, 0:8, :]
                second_ref[:, second_col + off : second_col + off + 128] = self.last[core, high, unit, 8:16, :]

    def close(self):
        for stage, ref in self.sent:
            wait_all(ref, self.send_sem.at[stage])

    def _y_cols(self, dy=0):
        return pl.ds(pl.multiple_of((self.t.y + dy) % 4 // 2 * 128, 128), 128)

    def spread(self):
        t = self.t
        self.core_total()
        for d in (2, 1, 3):
            self._copy(self.half.at[:, 0:4, (t.x + d) % 4], self.x_in.at[3 - d], X, t.in_plane(d, 0))
            self._copy(
                self.half.at[:, 4:8, :, (t.y + d) % 2, :, self._y_cols(d)], self.y_in.at[3 - d], Y, t.in_plane(0, d)
            )

    def turn(self):
        t = self.t
        self._arrived(X, self.x_in)
        total = self.half[:, 0:4, t.x].astype(F32)
        for slot in range(3):
            total = total + self.x_in[slot].astype(F32)
        self.x_sum[...] = total.astype(BF16)
        for d in (2, 1, 3):
            self._copy(
                self.x_sum.at[:, :, (t.y + d) % 2, :, self._y_cols(d)], self.xy_in.at[3 - d], XY, t.in_plane(0, d)
            )
        self._arrived(Y, self.y_in)
        total = self.half[:, 4:8, :, t.y % 2, :, self._y_cols()].astype(F32)
        for slot in range(3):
            total = total + self.y_in[slot].astype(F32)
        self.y_sum[...] = total.astype(BF16)
        for d in (2, 1, 3):
            self._copy(self.y_sum.at[:, :, (t.x + d) % 4], self.yx_in.at[3 - d], YX, t.in_plane(d, 0))

    def plane_total(self, sum_ref, place):
        t = self.t
        self._arrived(XY, self.xy_in)
        total = self.x_sum[:, :, t.y % 2, :, self._y_cols()].astype(F32)
        for slot in range(3):
            total = total + self.xy_in[slot].astype(F32)
        for unit in range(self.n):
            sum_ref[0:4, place + unit] = total[unit].astype(BF16)
        self._arrived(YX, self.yx_in)
        total = self.y_sum[:, :, t.x].astype(F32)
        for slot in range(3):
            total = total + self.yx_in[slot].astype(F32)
        for unit in range(self.n):
            sum_ref[4:8, place + unit] = total[unit].astype(BF16)


class Column:
    def __init__(self, torus, groups, sum_ref, in_ref, send_sem, recv_sem):
        self.t, self.groups, self.sum, self.came = torus, groups, sum_ref, in_ref
        self.send_sem, self.recv_sem = send_sem, recv_sem

    def send(self):
        t = self.t
        for dz, dh in COLUMN:
            slot = (-dz) % 8 * 2 + dh - 1
            pltpu.make_async_remote_copy(
                src_ref=self.sum.at[(t.z + dz) % 8],
                dst_ref=self.came.at[slot],
                send_sem=self.send_sem,
                recv_sem=self.recv_sem,
                device_id=t.in_column(dz, dh),
                device_id_type=MESH,
            ).start()

    def total(self):
        t = self.t
        wait_all(self.came, self.recv_sem)
        mine = self.sum[t.z].astype(F32)
        for dz in range(1, 8):
            mine = mine + self.came[dz * 2 - 1].astype(F32)
        other = self.came[0].astype(F32)
        for dz in range(1, 8):
            other = other + self.came[dz * 2].astype(F32)
        high = t.y // 2
        place = 0
        for group in self.groups:
            group.last[t.core, high] = mine[place : place + group.n]
            group.last[t.core, 1 - high] = other[place : place + group.n]
            group.send_last()
            place += group.n

    def close(self):
        wait_all(self.came, self.send_sem)


def kernel(
    tokens_hbm,
    land_hbm,
    pole_ref,
    land_vec_hbm,
    pole_vec_hbm,
    w1_hbm,
    o1_hbm,
    w2_hbm,
    o2_hbm,
    cot_hbm,
    layer_ref,
    tokens_grad_ref,
    ga1_ref,
    go1_ref,
    ga2_ref,
    go2_ref,
    *scratch,
):
    n = len(BLOCK_SCRATCH)
    one, two = Block(scratch[:n]), Block(scratch[n : 2 * n])
    rest = list(scratch[2 * n :])
    unit_refs = [[rest.pop(0) for _ in group_scratch(n)] for n in GROUPS]
    (tokens_ref, cot_ref, land_ref, land_vec_ref, pole_vec_ref, w1_ref, o1_ref, w2_ref, o2_ref, cells_ref, mask_ref,
     sum2, sum1, came2, came1, halo_out, halo_in, load_sem, halo_send, halo_recv, red_send, red_recv, col_send,
     col_recv) = rest

    torus = Torus()
    loads = [
        pltpu.make_async_copy(src, dst, load_sem.at[i])
        for i, (src, dst) in enumerate(
            (
                (tokens_hbm, tokens_ref),
                (land_hbm, land_ref),
                (land_vec_hbm, land_vec_ref),
                (pole_vec_hbm, pole_vec_ref),
                (w1_hbm, w1_ref),
                (o1_hbm, o1_ref),
                (cot_hbm, cot_ref),
                (w2_hbm, w2_ref),
                (o2_hbm, o2_ref),
            )
        )
    ]
    for load in loads:
        load.start()

    barrier = pltpu.get_barrier_semaphore()
    greeted = torus.greeted()
    for device in greeted:
        pl.semaphore_signal(barrier, inc=1, device_id=device, device_id_type=MESH)

    for load in loads[:4]:
        load.wait()
    land = land_ref[...].astype(F32)
    at_cell = lax.broadcasted_iota(jnp.int32, (WLON, 1, WLON), 0)
    eye = at_cell == lax.broadcasted_iota(jnp.int32, (WLON, 1, WLON), 2)
    land_vec = land_vec_ref[...].astype(F32).reshape(1, 1, D)
    pole_vec = pole_vec_ref[...].astype(F32).reshape(1, 1, D)

    def mark(chunk, row, side):
        row_marks = jnp.broadcast_to(land[row : row + 1, :].reshape(1, 1, WLON), (WLON, 1, WLON))
        column = jnp.sum(jnp.where(eye, row_marks, 0.0), axis=2, keepdims=True)[side * 6 : side * 6 + 6]
        marked = chunk + column * land_vec + pole_ref[row].astype(F32) * pole_vec
        return marked.astype(BF16).astype(F32)

    field_to_cells(tokens_ref, one.u, mark)
    halos = [
        Halo(torus, i, sign, halo_out, halo_in, halo_send, halo_recv) for i, sign in enumerate((-1, -1, 1, 1))
    ]
    both2, both1 = (
        Group(torus, n, refs, red_send.at[i], red_recv.at[i]) for i, (n, refs) in enumerate(zip(GROUPS, unit_refs))
    )
    column2 = Column(torus, [both2], sum2, came2, col_send.at[0], col_recv.at[0])
    column1 = Column(torus, [both1], sum1, came1, col_send.at[1], col_recv.at[1])

    loads[4].wait()
    loads[5].wait()
    first = forward(one, w1_ref, o1_ref, None)
    two.u[...] = first.astype(BF16).astype(F32)

    pl.semaphore_wait(barrier, len(greeted))
    halos[0].send(two.u)
    loads[6].wait()
    field_to_cells(cot_ref, two.dy)
    halos[1].send(two.dy)

    last = jnp.where(torus.lat == 63, 1.0, 0.0).astype(F32)
    far_k = (lax.broadcasted_iota(jnp.int32, (CELLS, CELLS), 0) // QUAD) % 2
    far_q = (lax.broadcasted_iota(jnp.int32, (CELLS, CELLS), 1) // QUAD) % 2
    mask_ref[...] = 1.0 - last * jnp.where(far_k == far_q, 0.0, 1.0)

    loads[7].wait()
    loads[8].wait()
    halos[0].receive(two.u)
    cells_ref[...] = forward(two, w2_ref, o2_ref, mask_ref)
    halos[2].send(cells_ref)
    halos[1].receive(two.dy)

    backward_mixed(two, o2_ref)
    backward_values(two)
    backward_scores(two, range(HEADS))
    one.dy[...] = backward_input(two, w2_ref)
    halos[3].send(one.dy)
    both2.start(0, output_and_value_unit(two))
    both2.start(1, query_and_key_unit(two))
    both2.spread()

    halos[3].receive(one.dy)
    backward_mixed(one, o1_ref)
    backward_scores(one, range(HEADS))
    both1.start(0, query_and_key_unit(one))
    backward_values(one)
    both1.start(1, output_and_value_unit(one))
    both1.spread()

    halos[2].receive(cells_ref)
    cells_to_field(cells_ref, layer_ref)
    cells_ref[...] = backward_input(one, w1_ref)
    cells_to_field(cells_ref, tokens_grad_ref)
    both2.turn()

    both1.turn()
    both2.plane_total(sum2, 0)
    column2.send()
    both1.plane_total(sum1, 0)
    column1.send()
    column2.total()
    both2.finish(0, go2_ref, 0, ga2_ref, 2 * D)
    both2.finish(1, ga2_ref, 0, ga2_ref, D)
    column1.total()
    both1.finish(0, ga1_ref, 0, ga1_ref, D)
    both1.finish(1, go1_ref, 0, ga1_ref, 2 * D)
    for each in halos + [both2, both1, column2, column1]:
        each.close()


def hand_over(*refs):
    for i in range(6):
        refs[6 + i][...] = refs[i][...]


def local(
    tokens,
    land_sea,
    pole_band,
    land_embedding,
    pole_embedding,
    attend_first,
    output_first,
    attend_second,
    output_second,
    cotangent,
):
    vmem = pl.BlockSpec(memory_space=pltpu.VMEM)
    smem = pl.BlockSpec(memory_space=pltpu.SMEM)
    hbm = pl.BlockSpec(memory_space=pl.ANY)
    field = jax.ShapeDtypeStruct((WLAT, WLON, LV, D), BF16)
    shapes = (
        field,
        field,
        jax.ShapeDtypeStruct((8, 3 * D), F32),
        jax.ShapeDtypeStruct((8, D), F32),
        jax.ShapeDtypeStruct((8, 3 * D), F32),
        jax.ShapeDtypeStruct((8, D), F32),
    )
    results = pl.pallas_call(
        kernel,
        out_shape=shapes,
        in_specs=[hbm, hbm, smem, hbm, hbm, hbm, hbm, hbm, hbm, hbm],
        out_specs=[vmem] * 6,
        scratch_shapes=[pltpu.VMEM(shape, dtype) for _, shape, dtype in BLOCK_SCRATCH * 2 + sum((group_scratch(n) for n in GROUPS), ())]
        + [
            pltpu.VMEM((WLAT, WLON, LV, D), BF16),
            pltpu.VMEM((WLAT, WLON, LV, D), BF16),
            pltpu.VMEM((WLAT, WLON), jnp.int32),
            pltpu.VMEM((D,), BF16),
            pltpu.VMEM((D,), BF16),
            pltpu.VMEM((D, 3 * D), BF16),
            pltpu.VMEM((D, D), BF16),
            pltpu.VMEM((D, 3 * D), BF16),
            pltpu.VMEM((D, D), BF16),
            pltpu.VMEM((CELLS, D), F32),
            pltpu.VMEM((CELLS, CELLS), F32),
            pltpu.VMEM((NZ, 2, 16, 128), BF16),
            pltpu.VMEM((NZ, 2, 16, 128), BF16),
            pltpu.VMEM((15, 2, 16, 128), BF16),
            pltpu.VMEM((15, 2, 16, 128), BF16),
            pltpu.VMEM((4, 3, SLAB, D), BF16),
            pltpu.VMEM((4, 3, SLAB, D), BF16),
            pltpu.SemaphoreType.DMA((9,)),
            pltpu.SemaphoreType.DMA((4,)),
            pltpu.SemaphoreType.DMA((4,)),
            pltpu.SemaphoreType.DMA((2, UNIT_SEMS)),
            pltpu.SemaphoreType.DMA((2, UNIT_SEMS)),
            pltpu.SemaphoreType.DMA((2,)),
            pltpu.SemaphoreType.DMA((2,)),
        ],
        compiler_params=pltpu.CompilerParams(
            collective_id=0, has_side_effects=True, vmem_limit_bytes=56 * 1024 * 1024
        ),
    )(
        tokens.transpose(1, 2, 0, 3),
        land_sea,
        pole_band,
        land_embedding,
        pole_embedding,
        attend_first,
        output_first,
        attend_second,
        output_second,
        cotangent.transpose(1, 2, 0, 3),
    )
    results = pl.pallas_call(
        hand_over,
        out_shape=shapes,
        in_specs=[vmem] * 6,
        out_specs=[vmem] * 6,
    )(*results)
    return tuple(r.transpose(2, 0, 1, 3) for r in results[:2]) + tuple(results[2:])


def solution(mesh):
    placed = (
        P(None, "lat", "lon", None),
        P("lat", "lon"),
        P("lat"),
        P(),
        P(),
        P(),
        P(),
        P(),
        P(),
        P(None, "lat", "lon", None),
    )
    return jax.shard_map(
        local,
        mesh=mesh,
        in_specs=placed,
        out_specs=(
            P(None, "lat", "lon", None),
            P(None, "lat", "lon", None),
            P("lat", None),
            P("lat", None),
            P("lat", None),
            P("lat", None),
        ),
        check_vma=False,
    )
```

```python
import functools
import math

import jax
import jax.numpy as jnp
from jax import lax
from jax.experimental import pallas as pl
from jax.experimental.pallas import tpu as pltpu
from jax.sharding import PartitionSpec as P

MESH = pl.DeviceIdType.MESH
BF16 = jnp.bfloat16
F32 = jnp.float32

D = 512
HEADS = 16
PER_HEAD = D // HEADS
LV = 2
WLAT = 6
WLON = 12
CELLS = LV * WLAT * WLON
QUAD = CELLS // 4
SLAB = 48
EPS = 1e-05
SCALE = 1.0 / math.sqrt(PER_HEAD)
EXP2_SCALE = SCALE * math.log2(math.e)

NZ, NX, NYL = 8, 4, 2
COLUMN = [(dz, dh) for dz in (4, 3, 5, 2, 6, 1, 7, 0) for dh in (1, 0) if (dz, dh) != (0, 0)]


def mm(left, right):
    return lax.dot_general(left, right, (((1,), (0,)), ((), ())), preferred_element_type=F32)


def mm_nt(left, right):
    return lax.dot_general(left, right, (((1,), (1,)), ((), ())), preferred_element_type=F32)


def chunk_offset(row, side):
    quadrant = (0 if row >= 3 else 1) + (0 if side == 1 else 2)
    return quadrant * QUAD + row % 3 * 12


def field_to_cells(field_ref, cells_ref, change=lambda chunk, row, side: chunk):
    for row in range(WLAT):
        for side in range(2):
            off = chunk_offset(row, side)
            chunk = field_ref[row, side * 6 : side * 6 + 6, :, :].astype(F32)
            cells_ref[off : off + 12, :] = change(chunk, row, side).reshape(12, D)


def cells_to_field(cells_ref, field_ref):
    for row in range(WLAT):
        for side in range(2):
            off = chunk_offset(row, side)
            field_ref[row, side * 6 : side * 6 + 6, :, :] = cells_ref[off : off + 12, :].reshape(6, LV, D).astype(BF16)


def layer_norm(u):
    centre = jnp.mean(u, axis=-1, keepdims=True)
    centred = u - centre
    spread = lax.rsqrt(jnp.mean(centred * centred, axis=-1, keepdims=True) + EPS)
    return centred * spread, spread


def head_lanes(head):
    lane = lax.broadcasted_iota(jnp.int32, (CELLS, 256), 1)
    return (lane // PER_HEAD) == (head % 8)


def head_rows(part, head):
    first = part * D + head * PER_HEAD
    return slice(first, first + PER_HEAD)


def forward(blk, w_ref, wo_ref, mask_ref):
    u = blk.u[...]
    normed, spread = layer_norm(u)
    blk.normed[...] = normed
    blk.spread[...] = jnp.broadcast_to(spread, (CELLS, 128))
    hidden = normed.astype(BF16)
    blk.hid_t[...] = hidden.T
    for part in range(3):
        cols = slice(part * D, part * D + D)
        packed = mm(hidden, w_ref[:, cols]).astype(BF16)
        blk.pk[:, cols] = packed
        blk.pk_t[cols, :] = packed.T

    def one_head(head):
        group = head // 8
        q_g = blk.pk[:, group * 256 : group * 256 + 256]
        k_g = blk.pk[:, D + group * 256 : D + group * 256 + 256]
        k_h = jnp.where(head_lanes(head), k_g, jnp.zeros_like(k_g))
        weights = jnp.exp2(mm_nt(k_h, q_g) * EXP2_SCALE)
        if mask_ref is not None:
            weights = weights * mask_ref[...]
        attention = (weights * (1.0 / jnp.sum(weights, axis=0, keepdims=True))).astype(BF16)
        blk.att[head] = attention

    for head in range(HEADS):
        one_head(head)
    for head in range(HEADS):
        blk.mix_t[head_rows(0, head), :] = mm(blk.pk_t[head_rows(2, head), :], blk.att[head])
    mixed = blk.mix_t[...].astype(BF16).T
    return u + mm(mixed, wo_ref[...])


def backward_mixed(blk, wo_ref):
    dy_low = blk.dy[...].astype(BF16)
    blk.gm[...] = mm_nt(dy_low, wo_ref[...]).astype(BF16)
    blk.gm_t[...] = blk.gm[...].T


def backward_values(blk):
    for head in range(HEADS):
        g_t = blk.gm_t[head_rows(0, head), :]
        blk.dpk_t[head_rows(2, head), :] = mm_nt(g_t, blk.att[head]).astype(BF16)


def backward_scores(blk, heads):
    for head in heads:
        group = head // 8
        v_g = blk.pk[:, 2 * D + group * 256 : 2 * D + group * 256 + 256]
        g_g = blk.gm[:, group * 256 : group * 256 + 256]
        v_h = jnp.where(head_lanes(head), v_g, jnp.zeros_like(v_g))
        grad_attention = mm_nt(v_h, g_g)
        rows = head_rows(0, head)
        inner = jnp.sum(blk.mix_t[rows, :] * blk.gm_t[rows, :].astype(F32), axis=0, keepdims=True)
        blk.dsc[head] = (blk.att[head].astype(F32) * (grad_attention - inner)).astype(BF16)
    for head in heads:
        rows, key_rows = head_rows(0, head), head_rows(1, head)
        grad_scores = blk.dsc[head]
        blk.dpk_t[rows, :] = (mm(blk.pk_t[key_rows, :], grad_scores) * SCALE).astype(BF16)
        blk.dpk_t[key_rows, :] = (mm_nt(blk.pk_t[rows, :], grad_scores) * SCALE).astype(BF16)


def backward_input(blk, w_ref):
    grad_hidden = mm(w_ref[...], blk.dpk_t[...]).T
    normed = blk.normed[...]
    spread = blk.spread[:, 0:1]
    return blk.dy[...] + spread * (
        grad_hidden
        - jnp.mean(grad_hidden, axis=-1, keepdims=True)
        - normed * jnp.mean(grad_hidden * normed, axis=-1, keepdims=True)
    )


def pack_unit(first, second):
    first = first.reshape(64, 8, D)
    second = second.reshape(64, 8, D)
    return jnp.concatenate([first, second], axis=1).astype(BF16).reshape(NZ, NX, NYL, 16, D)


def output_and_value_unit(blk):
    grad_output = mm(blk.mix_t[...].astype(BF16), blk.dy[...].astype(BF16))
    grad_value = mm_nt(blk.hid_t[...], blk.dpk_t[2 * D :, :])
    return pack_unit(grad_output, grad_value)


def query_and_key_unit(blk):
    hid_t = blk.hid_t[...]
    return pack_unit(mm_nt(hid_t, blk.dpk_t[0:D, :]), mm_nt(hid_t, blk.dpk_t[D : 2 * D, :]))


BLOCK_SCRATCH = (
    ("u", (CELLS, D), F32),
    ("normed", (CELLS, D), F32),
    ("spread", (CELLS, 128), F32),
    ("hid_t", (D, CELLS), BF16),
    ("pk", (CELLS, 3 * D), BF16),
    ("pk_t", (3 * D, CELLS), BF16),
    ("att", (HEADS, CELLS, CELLS), BF16),
    ("dsc", (HEADS, CELLS, CELLS), BF16),
    ("mix_t", (D, CELLS), F32),
    ("dy", (CELLS, D), F32),
    ("gm", (CELLS, D), BF16),
    ("gm_t", (D, CELLS), BF16),
    ("dpk_t", (3 * D, CELLS), BF16),
)


class Block:
    def __init__(self, refs):
        for (name, _, _), ref in zip(BLOCK_SCRATCH, refs):
            setattr(self, name, ref)


class Torus:
    def __init__(self):
        self.lat = lax.axis_index("lat")
        self.lon = lax.axis_index("lon")
        self.z = self.lat // 8
        self.x = (self.lat // 2) % 4
        self.y = (self.lon // 2) * 2 + self.lat % 2
        self.core = self.lon % 2

    def at(self, x=None, y=None, z=None, core=None):
        x = self.x if x is None else x
        y = self.y if y is None else y
        z = self.z if z is None else z
        core = self.core if core is None else core
        return (z * 8 + x * 2 + y % 2, (y // 2) * 2 + core)

    def shifted(self, dlat, dlon):
        return ((self.lat + dlat + 64) % 64, (self.lon + dlon + 4) % 4)

    def greeted(self):
        found = [self.shifted(*step) for step in ((1, 0), (-1, 0), (1, 1), (-1, -1), (0, 1), (0, -1))]
        found += [self.at(core=1 - self.core)]
        found += [self.in_plane(*step) for step in ((2, 0), (0, 2), (1, 0), (3, 0), (0, 1), (0, 3))]
        found += [self.in_column(dz, dh) for dz, dh in COLUMN]
        return found

    def in_plane(self, dx, dy):
        return self.at(x=(self.x + dx) % 4, y=(self.y + dy) % 4)

    def in_column(self, dz, dh):
        return self.at(z=(self.z + dz) % 8, y=(self.y + 2 * dh) % 4)


def wait_all(ref, sem):
    pltpu.make_async_copy(ref, ref, sem).wait()


class Halo:
    STEPS = ((1, 0), (0, 1), (1, 1))

    def __init__(self, torus, index, sign, out_ref, in_ref, send_sem, recv_sem):
        self.torus, self.sign = torus, sign
        self.out_ref, self.in_ref = out_ref.at[index], in_ref.at[index]
        self.send_sem, self.recv_sem = send_sem.at[index], recv_sem.at[index]

    def send(self, cells_ref):
        for n, (dlat, dlon) in enumerate(self.STEPS):
            q = n + 1
            self.out_ref[n, 0:QUAD, :] = cells_ref[q * QUAD : q * QUAD + QUAD, :].astype(BF16)
            pltpu.make_async_remote_copy(
                src_ref=self.out_ref.at[n],
                dst_ref=self.in_ref.at[n],
                send_sem=self.send_sem,
                recv_sem=self.recv_sem,
                device_id=self.torus.shifted(self.sign * dlat, self.sign * dlon),
                device_id_type=MESH,
            ).start()

    def receive(self, cells_ref):
        wait_all(self.in_ref, self.recv_sem)
        for n in range(3):
            q = n + 1
            cells_ref[q * QUAD : q * QUAD + QUAD, :] = self.in_ref[n, 0:QUAD, :].astype(F32)

    def close(self):
        wait_all(self.out_ref, self.send_sem)


def group_scratch(n):
    return (
        ("whole", (n, NZ, NX, NYL, 16, D), BF16),
        ("core_in", (n, NZ, NX, NYL, 16, 256), BF16),
        ("half", (n, NZ, NX, NYL, 16, 256), BF16),
        ("x_in", (3, n, 4, NYL, 16, 256), BF16),
        ("x_sum", (n, 4, NYL, 16, 256), BF16),
        ("y_in", (3, n, 4, NX, 16, 128), BF16),
        ("y_sum", (n, 4, NX, 16, 128), BF16),
        ("xy_in", (3, n, 4, 16, 128), BF16),
        ("yx_in", (3, n, 4, 16, 128), BF16),
        ("last", (2, 2, n, 16, 128), F32),
    )


GROUPS = (2, 2)
UNIT_SEMS = 6
CORE, X, Y, XY, YX, LAST = range(UNIT_SEMS)


class Group:
    def __init__(self, torus, n, refs, send_sem, recv_sem):
        self.t, self.n = torus, n
        for (name, _, _), ref in zip(group_scratch(n), refs):
            setattr(self, name, ref)
        self.send_sem, self.recv_sem = send_sem, recv_sem
        self.sent = []

    def _copy(self, src, dst, stage, device):
        pltpu.make_async_remote_copy(
            src_ref=src,
            dst_ref=dst,
            send_sem=self.send_sem.at[stage],
            recv_sem=self.recv_sem.at[stage],
            device_id=device,
            device_id_type=MESH,
        ).start()

    def _arrived(self, stage, ref):
        wait_all(ref, self.recv_sem.at[stage])
        self.sent.append((stage, ref))

    def start(self, unit, gradients):
        t = self.t
        self.whole[unit] = gradients
        cols = pl.ds(pl.multiple_of((1 - t.core) * 256, 256), 256)
        self._copy(self.whole.at[unit, :, :, :, :, cols], self.core_in.at[unit], CORE, t.at(core=1 - t.core))

    def core_total(self):
        self._arrived(CORE, self.core_in)
        cols = pl.ds(pl.multiple_of(self.t.core * 256, 256), 256)
        self.half[...] = self.whole[:, :, :, :, :, cols] + self.core_in[...]

    def send_last(self):
        t = self.t
        self._copy(self.last.at[t.core], self.last.at[t.core], LAST, t.at(core=1 - t.core))

    def finish(self, unit, first_ref, first_col, second_ref, second_col):
        if unit == 0:
            self._arrived(LAST, self.last.at[1 - self.t.core])
        for core in range(2):
            for high in range(2):
                off = core * 256 + high * 128
                first_ref[:, first_col + off : first_col + off + 128] = self.last[core, high, unit, 0:8, :]
                second_ref[:, second_col + off : second_col + off + 128] = self.last[core, high, unit, 8:16, :]

    def close(self):
        for stage, ref in self.sent:
            wait_all(ref, self.send_sem.at[stage])

    def _y_cols(self, dy=0):
        return pl.ds(pl.multiple_of((self.t.y + dy) % 4 // 2 * 128, 128), 128)

    def spread(self):
        t = self.t
        self.core_total()
        for d in (2, 1, 3):
            self._copy(self.half.at[:, 0:4, (t.x + d) % 4], self.x_in.at[3 - d], X, t.in_plane(d, 0))
            self._copy(
                self.half.at[:, 4:8, :, (t.y + d) % 2, :, self._y_cols(d)], self.y_in.at[3 - d], Y, t.in_plane(0, d)
            )

    def turn(self):
        t = self.t
        self._arrived(X, self.x_in)
        total = self.half[:, 0:4, t.x].astype(F32)
        for slot in range(3):
            total = total + self.x_in[slot].astype(F32)
        self.x_sum[...] = total.astype(BF16)
        for d in (2, 1, 3):
            self._copy(
                self.x_sum.at[:, :, (t.y + d) % 2, :, self._y_cols(d)], self.xy_in.at[3 - d], XY, t.in_plane(0, d)
            )
        self._arrived(Y, self.y_in)
        total = self.half[:, 4:8, :, t.y % 2, :, self._y_cols()].astype(F32)
        for slot in range(3):
            total = total + self.y_in[slot].astype(F32)
        self.y_sum[...] = total.astype(BF16)
        for d in (2, 1, 3):
            self._copy(self.y_sum.at[:, :, (t.x + d) % 4], self.yx_in.at[3 - d], YX, t.in_plane(d, 0))

    def plane_total(self, sum_ref, place):
        t = self.t
        self._arrived(XY, self.xy_in)
        total = self.x_sum[:, :, t.y % 2, :, self._y_cols()].astype(F32)
        for slot in range(3):
            total = total + self.xy_in[slot].astype(F32)
        for unit in range(self.n):
            sum_ref[0:4, place + unit] = total[unit].astype(BF16)
        self._arrived(YX, self.yx_in)
        total = self.y_sum[:, :, t.x].astype(F32)
        for slot in range(3):
            total = total + self.yx_in[slot].astype(F32)
        for unit in range(self.n):
            sum_ref[4:8, place + unit] = total[unit].astype(BF16)


class Column:
    def __init__(self, torus, groups, sum_ref, in_ref, send_sem, recv_sem):
        self.t, self.groups, self.sum, self.came = torus, groups, sum_ref, in_ref
        self.send_sem, self.recv_sem = send_sem, recv_sem

    def send(self):
        t = self.t
        for dz, dh in COLUMN:
            slot = (-dz) % 8 * 2 + dh - 1
            pltpu.make_async_remote_copy(
                src_ref=self.sum.at[(t.z + dz) % 8],
                dst_ref=self.came.at[slot],
                send_sem=self.send_sem,
                recv_sem=self.recv_sem,
                device_id=t.in_column(dz, dh),
                device_id_type=MESH,
            ).start()

    def total(self):
        t = self.t
        wait_all(self.came, self.recv_sem)
        mine = self.sum[t.z].astype(F32)
        for dz in range(1, 8):
            mine = mine + self.came[dz * 2 - 1].astype(F32)
        other = self.came[0].astype(F32)
        for dz in range(1, 8):
            other = other + self.came[dz * 2].astype(F32)
        high = t.y // 2
        place = 0
        for group in self.groups:
            group.last[t.core, high] = mine[place : place + group.n]
            group.last[t.core, 1 - high] = other[place : place + group.n]
            group.send_last()
            place += group.n

    def close(self):
        wait_all(self.came, self.send_sem)


def kernel(
    tokens_hbm,
    land_hbm,
    pole_ref,
    land_vec_hbm,
    pole_vec_hbm,
    w1_hbm,
    o1_hbm,
    w2_hbm,
    o2_hbm,
    cot_hbm,
    layer_ref,
    tokens_grad_ref,
    ga1_ref,
    go1_ref,
    ga2_ref,
    go2_ref,
    *scratch,
):
    n = len(BLOCK_SCRATCH)
    one, two = Block(scratch[:n]), Block(scratch[n : 2 * n])
    rest = list(scratch[2 * n :])
    unit_refs = [[rest.pop(0) for _ in group_scratch(n)] for n in GROUPS]
    (tokens_ref, cot_ref, land_ref, land_vec_ref, pole_vec_ref, w1_ref, o1_ref, w2_ref, o2_ref, cells_ref, mask_ref,
     sum2, sum1, came2, came1, halo_out, halo_in, load_sem, halo_send, halo_recv, red_send, red_recv, col_send,
     col_recv) = rest

    torus = Torus()
    loads = [
        pltpu.make_async_copy(src, dst, load_sem.at[i])
        for i, (src, dst) in enumerate(
            (
                (tokens_hbm, tokens_ref),
                (land_hbm, land_ref),
                (land_vec_hbm, land_vec_ref),
                (pole_vec_hbm, pole_vec_ref),
                (w1_hbm, w1_ref),
                (o1_hbm, o1_ref),
                (cot_hbm, cot_ref),
                (w2_hbm, w2_ref),
                (o2_hbm, o2_ref),
            )
        )
    ]
    for load in loads:
        load.start()

    barrier = pltpu.get_barrier_semaphore()
    greeted = torus.greeted()
    for device in greeted:
        pl.semaphore_signal(barrier, inc=1, device_id=device, device_id_type=MESH)

    for load in loads[:4]:
        load.wait()
    land = land_ref[...].astype(F32)
    at_cell = lax.broadcasted_iota(jnp.int32, (WLON, 1, WLON), 0)
    eye = at_cell == lax.broadcasted_iota(jnp.int32, (WLON, 1, WLON), 2)
    land_vec = land_vec_ref[...].astype(F32).reshape(1, 1, D)
    pole_vec = pole_vec_ref[...].astype(F32).reshape(1, 1, D)

    def mark(chunk, row, side):
        row_marks = jnp.broadcast_to(land[row : row + 1, :].reshape(1, 1, WLON), (WLON, 1, WLON))
        column = jnp.sum(jnp.where(eye, row_marks, 0.0), axis=2, keepdims=True)[side * 6 : side * 6 + 6]
        marked = chunk + column * land_vec + pole_ref[row].astype(F32) * pole_vec
        return marked.astype(BF16).astype(F32)

    field_to_cells(tokens_ref, one.u, mark)
    halos = [
        Halo(torus, i, sign, halo_out, halo_in, halo_send, halo_recv) for i, sign in enumerate((-1, -1, 1, 1))
    ]
    both2, both1 = (
        Group(torus, n, refs, red_send.at[i], red_recv.at[i]) for i, (n, refs) in enumerate(zip(GROUPS, unit_refs))
    )
    column2 = Column(torus, [both2], sum2, came2, col_send.at[0], col_recv.at[0])
    column1 = Column(torus, [both1], sum1, came1, col_send.at[1], col_recv.at[1])

    loads[4].wait()
    loads[5].wait()
    first = forward(one, w1_ref, o1_ref, None)
    two.u[...] = first.astype(BF16).astype(F32)

    pl.semaphore_wait(barrier, len(greeted))
    halos[0].send(two.u)
    loads[6].wait()
    field_to_cells(cot_ref, two.dy)
    halos[1].send(two.dy)

    last = jnp.where(torus.lat == 63, 1.0, 0.0).astype(F32)
    far_k = (lax.broadcasted_iota(jnp.int32, (CELLS, CELLS), 0) // QUAD) % 2
    far_q = (lax.broadcasted_iota(jnp.int32, (CELLS, CELLS), 1) // QUAD) % 2
    mask_ref[...] = 1.0 - last * jnp.where(far_k == far_q, 0.0, 1.0)

    loads[7].wait()
    loads[8].wait()
    halos[0].receive(two.u)
    cells_ref[...] = forward(two, w2_ref, o2_ref, mask_ref)
    halos[1].receive(two.dy)

    backward_mixed(two, o2_ref)
    backward_values(two)
    backward_scores(two, range(HEADS))
    one.dy[...] = backward_input(two, w2_ref)
    halos[3].send(one.dy)
    both2.start(0, output_and_value_unit(two))
    both2.start(1, query_and_key_unit(two))
    both2.spread()

    halos[3].receive(one.dy)
    backward_mixed(one, o1_ref)
    backward_scores(one, range(HEADS))
    both1.start(0, query_and_key_unit(one))
    backward_values(one)
    both1.start(1, output_and_value_unit(one))
    halos[2].send(cells_ref)
    both1.spread()

    two.u[...] = backward_input(one, w1_ref)
    cells_to_field(two.u, tokens_grad_ref)
    both2.turn()

    both1.turn()
    halos[2].receive(cells_ref)
    cells_to_field(cells_ref, layer_ref)
    both2.plane_total(sum2, 0)
    column2.send()
    both1.plane_total(sum1, 0)
    column1.send()
    column2.total()
    both2.finish(0, go2_ref, 0, ga2_ref, 2 * D)
    both2.finish(1, ga2_ref, 0, ga2_ref, D)
    column1.total()
    both1.finish(0, ga1_ref, 0, ga1_ref, D)
    both1.finish(1, go1_ref, 0, ga1_ref, 2 * D)
    for each in halos + [both2, both1, column2, column1]:
        each.close()


def hand_over(*refs):
    for i in range(6):
        refs[6 + i][...] = refs[i][...]


def local(
    tokens,
    land_sea,
    pole_band,
    land_embedding,
    pole_embedding,
    attend_first,
    output_first,
    attend_second,
    output_second,
    cotangent,
):
    vmem = pl.BlockSpec(memory_space=pltpu.VMEM)
    smem = pl.BlockSpec(memory_space=pltpu.SMEM)
    hbm = pl.BlockSpec(memory_space=pl.ANY)
    field = jax.ShapeDtypeStruct((WLAT, WLON, LV, D), BF16)
    shapes = (
        field,
        field,
        jax.ShapeDtypeStruct((8, 3 * D), F32),
        jax.ShapeDtypeStruct((8, D), F32),
        jax.ShapeDtypeStruct((8, 3 * D), F32),
        jax.ShapeDtypeStruct((8, D), F32),
    )
    results = pl.pallas_call(
        kernel,
        out_shape=shapes,
        in_specs=[hbm, hbm, smem, hbm, hbm, hbm, hbm, hbm, hbm, hbm],
        out_specs=[vmem] * 6,
        scratch_shapes=[pltpu.VMEM(shape, dtype) for _, shape, dtype in BLOCK_SCRATCH * 2 + sum((group_scratch(n) for n in GROUPS), ())]
        + [
            pltpu.VMEM((WLAT, WLON, LV, D), BF16),
            pltpu.VMEM((WLAT, WLON, LV, D), BF16),
            pltpu.VMEM((WLAT, WLON), jnp.int32),
            pltpu.VMEM((D,), BF16),
            pltpu.VMEM((D,), BF16),
            pltpu.VMEM((D, 3 * D), BF16),
            pltpu.VMEM((D, D), BF16),
            pltpu.VMEM((D, 3 * D), BF16),
            pltpu.VMEM((D, D), BF16),
            pltpu.VMEM((CELLS, D), F32),
            pltpu.VMEM((CELLS, CELLS), F32),
            pltpu.VMEM((NZ, 2, 16, 128), BF16),
            pltpu.VMEM((NZ, 2, 16, 128), BF16),
            pltpu.VMEM((15, 2, 16, 128), BF16),
            pltpu.VMEM((15, 2, 16, 128), BF16),
            pltpu.VMEM((4, 3, SLAB, D), BF16),
            pltpu.VMEM((4, 3, SLAB, D), BF16),
            pltpu.SemaphoreType.DMA((9,)),
            pltpu.SemaphoreType.DMA((4,)),
            pltpu.SemaphoreType.DMA((4,)),
            pltpu.SemaphoreType.DMA((2, UNIT_SEMS)),
            pltpu.SemaphoreType.DMA((2, UNIT_SEMS)),
            pltpu.SemaphoreType.DMA((2,)),
            pltpu.SemaphoreType.DMA((2,)),
        ],
        compiler_params=pltpu.CompilerParams(
            collective_id=0, has_side_effects=True, vmem_limit_bytes=56 * 1024 * 1024
        ),
    )(
        tokens.transpose(1, 2, 0, 3),
        land_sea,
        pole_band,
        land_embedding,
        pole_embedding,
        attend_first,
        output_first,
        attend_second,
        output_second,
        cotangent.transpose(1, 2, 0, 3),
    )
    results = pl.pallas_call(
        hand_over,
        out_shape=shapes,
        in_specs=[vmem] * 6,
        out_specs=[vmem] * 6,
    )(*results)
    return tuple(r.transpose(2, 0, 1, 3) for r in results[:2]) + tuple(results[2:])


def solution(mesh):
    placed = (
        P(None, "lat", "lon", None),
        P("lat", "lon"),
        P("lat"),
        P(),
        P(),
        P(),
        P(),
        P(),
        P(),
        P(None, "lat", "lon", None),
    )
    return jax.shard_map(
        local,
        mesh=mesh,
        in_specs=placed,
        out_specs=(
            P(None, "lat", "lon", None),
            P(None, "lat", "lon", None),
            P("lat", None),
            P("lat", None),
            P("lat", None),
            P("lat", None),
        ),
        check_vma=False,
    )
```
